512 devices in a mesh: section: 8 (over z), expert: 32 (over y, x), dp: 2 (over core).
Axes of the slice: x: 4, y: 8, z: 8, core: 2. Of those that a mesh axis runs over, the one named last changes fastest.
Arguments:
- blocks: bfloat16 [8, 8192, 3072], P('section', ('dp', 'expert')), parts along dimension 1, may hold values from -6 to 6
- norm_gain: bfloat16 [8, 3072], P('section'), may hold values from 0.25 to 1.75
- w_gate: bfloat16 [8, 3072, 6144], P('section', None, 'expert'), may hold values from -0.109375 to 0.109375
- w_up: bfloat16 [8, 3072, 6144], P('section', None, 'expert'), may hold values from -0.109375 to 0.109375
- w_down: bfloat16 [8, 6144, 3072], P('section', 'expert'), may hold values from -0.15625 to 0.15625
- route_ids: int32 [8, 8192, 2], P('section', ('dp', 'expert')), parts along dimension 1, may hold values from 0 to 11, as said below
- route_weights: float32 [8, 8192, 2], P('section', ('dp', 'expert')), parts along dimension 1, may hold values from 0.05 to 1
Outputs:
- mixed: bfloat16 [8, 8192, 3072], P('section', ('dp', 'expert')), parts along dimension 1
The draws below stay inside these ranges and needn't reach their ends.
There are 2 independent parts, one for each index of `dp`. The reference program is written for one: setup_inputs(seed, part) draws one part's arguments, and reference() takes and returns one part's arrays. A program takes and returns all parts, laid end to end along the dimension named above; an argument that names none is the same for every part. Nothing has to cross between parts.
Inputs may be any that keep to these rules, and one draw needn't show every extreme that they name: `route_ids`: each token names 2 different ids. Within each aligned block of 128 tokens of a section (the tokens of one device), every computing expert (ids below 4) is named exactly 32 times and every zero-computation id at most 32 times.
All inputs are finite; a program needn't handle non-finite values.
Results may differ from the reference program's by a relative error of at most 0.0085.
Values may be sent and summed in bfloat16 or wider, within the bound.
A program may use at most 64 MiB of HBM per device.

```python
import jax
import jax.numpy as jnp
from jax import lax

D = 3072
HID = 1536
HSLICE = 192
EXPERTS = 4
ZEROS = 8
TOPK = 2
TOK_DEV = 128
CAP = 32
TOKENS = 4096
N_SECTION = 8
N_EXPERT = 32


def route_plan(key):
    block_count = N_SECTION * N_EXPERT
    block_keys = jax.random.split(jax.random.fold_in(key, 11), block_count)
    ranks = jax.vmap(lambda k: jax.random.permutation(k, TOK_DEV))(block_keys).astype(jnp.int32)
    offset = jax.random.randint(jax.random.fold_in(key, 12), (block_count, 1), 0, ZEROS).astype(jnp.int32)
    flips = jax.random.randint(jax.random.fold_in(key, 13), (block_count, TOK_DEV), 0, 2).astype(jnp.int32)
    computing = ranks < EXPERTS * CAP
    comp_id = (ranks // CAP).astype(jnp.int32)
    zero_second = (EXPERTS + (ranks + offset) % ZEROS).astype(jnp.int32)
    zero_first = (EXPERTS + (ranks + offset + ZEROS // 2) % ZEROS).astype(jnp.int32)
    first = jnp.where(computing, comp_id, zero_first).astype(jnp.int32)
    pick_one = jnp.where(flips == 1, zero_second, first).astype(jnp.int32)
    pick_two = jnp.where(flips == 1, first, zero_second).astype(jnp.int32)
    ids = jnp.stack([pick_one, pick_two], axis=-1).reshape(N_SECTION, TOKENS, TOPK)
    return (ids.astype(jnp.int32), ids < EXPERTS)


def draw_route_ids(key, part):
    ids, computing = route_plan(key)
    return ids


def draw_route_weights(key, part):
    ids, computing = route_plan(key)
    key = jax.random.fold_in(key, 7)
    uniform_draw = jax.random.uniform(key, (N_SECTION, TOKENS, TOPK), jnp.float32)
    comp_weight = 0.5 + 0.5 * uniform_draw
    zero_weight = jnp.exp(jnp.log(0.05) + uniform_draw * jnp.log(20.0))
    return jnp.clip(jnp.where(computing, comp_weight, zero_weight), 0.05, 1.0).astype(jnp.float32)


def block_scale(own_key, extent, cuts, low, high):
    def one(dim, parts):
        steps = jax.random.uniform(jax.random.fold_in(jax.random.fold_in(own_key, 6), dim), (parts,), jnp.float32, low / len(cuts), high / len(cuts))
        return jnp.repeat(jnp.exp(steps), extent[dim] // parts).reshape((-1,) + (1,) * (len(extent) - dim - 1))

    level = one(*cuts[0])
    for cut in cuts[1:]:
        level = level * one(*cut)
    return level


def gaussian(own_key, dims, spread, bound, pieces=(), kind=jnp.bfloat16):
    drawn = spread * jax.random.normal(own_key, dims, jnp.float32)
    if pieces:
        drawn = drawn * block_scale(own_key, dims, pieces, -0.22, 0.18)
    return jnp.clip(drawn, -bound, bound).astype(kind)


def setup_inputs(seed: int = 0, part: int = 0) -> dict:
    key_list = jax.random.split(jax.random.key(seed), 8)
    part_keys = jax.random.split(jax.random.fold_in(key_list[7], part), 8)
    blocks = gaussian(part_keys[0], (N_SECTION, TOKENS, D), 1.0, 6.0, ((0, 8), (1, 32)))
    norm_gain = jnp.clip(1.0 + 0.15 * jax.random.normal(key_list[1], (N_SECTION, D), jnp.float32), 0.25, 1.75).astype(jnp.bfloat16)
    w_gate = gaussian(key_list[2], (N_SECTION, D, EXPERTS * HID), D ** -0.5, 0.109375, ((0, 8), (2, 32)))
    w_up = gaussian(key_list[3], (N_SECTION, D, EXPERTS * HID), D ** -0.5, 0.109375, ((0, 8), (2, 32)))
    w_down = gaussian(key_list[4], (N_SECTION, EXPERTS * HID, D), HID ** -0.5, 0.15625, ((0, 8), (1, 32)))
    route_ids = draw_route_ids(jax.random.fold_in(jax.random.fold_in(key_list[7], part), 71), part)
    route_weights = draw_route_weights(jax.random.fold_in(jax.random.fold_in(key_list[7], part), 71), part)
    return dict(blocks=blocks, norm_gain=norm_gain, w_gate=w_gate, w_up=w_up, w_down=w_down, route_ids=route_ids, route_weights=route_weights)


def reference(blocks, norm_gain, w_gate, w_up, w_down, route_ids, route_weights):
    arrived = jnp.roll(blocks, 1, axis=0)
    slice_count = HID // HSLICE

    def one_section(section_args):
        block, section_gain, gate_full, up_full, down_full, section_ids, section_weights = section_args
        residual = block.astype(jnp.float32)
        inverse = lax.rsqrt(lax.optimization_barrier(jnp.mean(residual * residual, axis=-1, keepdims=True)) + 1e-06)
        normed = (residual * inverse * section_gain.astype(jnp.float32)).astype(jnp.bfloat16)
        token_rows = jnp.repeat(normed.reshape(N_EXPERT, TOK_DEV, D), TOPK, axis=1)
        pick_ids = section_ids.reshape(N_EXPERT, TOK_DEV * TOPK)
        pick_weights = section_weights.reshape(N_EXPERT, TOK_DEV * TOPK)
        zero_weight = lax.optimization_barrier(jnp.sum(jnp.where(section_ids >= EXPERTS, section_weights, 0.0), axis=1))
        start = residual + zero_weight[:, None] * normed.astype(jnp.float32)
        start = start.reshape(N_EXPERT, TOK_DEV, D)

        def fill(rows, target):
            return jnp.zeros((CAP + 1, D), jnp.bfloat16).at[target].set(rows)[:CAP]

        def one_expert(total, expert):
            member = pick_ids == expert
            slot_rank = (jnp.cumsum(member.astype(jnp.int32), axis=1) - 1).astype(jnp.int32)
            target = jnp.where(member, slot_rank, CAP).astype(jnp.int32)
            buffer = jax.vmap(fill)(token_rows, target).reshape(N_EXPERT * CAP, D)
            gate_cols = lax.dynamic_slice_in_dim(gate_full, (expert * HID).astype(jnp.int32), HID, 1)
            up_cols = lax.dynamic_slice_in_dim(up_full, (expert * HID).astype(jnp.int32), HID, 1)
            down_rows = lax.dynamic_slice_in_dim(down_full, (expert * HID).astype(jnp.int32), HID, 0)
            gate_act = jnp.dot(buffer, gate_cols, preferred_element_type=jnp.float32)
            up_act = jnp.dot(buffer, up_cols, preferred_element_type=jnp.float32)
            hidden = (jax.nn.silu(gate_act) * up_act).astype(jnp.bfloat16)
            hidden_split = hidden.astype(jnp.float32).reshape(N_EXPERT * CAP, slice_count, HSLICE)
            down_split = down_rows.astype(jnp.float32).reshape(slice_count, HSLICE, D)
            partial_value = jnp.einsum('rgk,gkd->grd', hidden_split, down_split)
            rounded = lax.optimization_barrier(partial_value.astype(jnp.bfloat16))
            expert_out = lax.optimization_barrier(jnp.sum(rounded.astype(jnp.float32), axis=0)).reshape(N_EXPERT, CAP, D)
            safe_rank = jnp.clip(slot_rank, 0, CAP - 1).astype(jnp.int32)
            taken = jnp.take_along_axis(expert_out, safe_rank[:, :, None], axis=1)
            scale = jnp.where(member, pick_weights, 0.0)
            added = (taken * scale[:, :, None]).reshape(N_EXPERT, TOK_DEV, TOPK, D)
            return (total + lax.optimization_barrier(jnp.sum(added, axis=2)), None)
        total, unused = lax.scan(one_expert, start, jnp.arange(EXPERTS, dtype=jnp.int32))
        return total.reshape(TOKENS, D).astype(jnp.bfloat16)
    return lax.map(one_section, (arrived, norm_gain, w_gate, w_up, w_down, route_ids, route_weights))
```

```python
import jax
import jax.numpy as jnp
from jax import lax
from jax.experimental import pallas as pl
from jax.experimental.pallas import tpu as pltpu
from jax.sharding import PartitionSpec as P

D = 3072
HS = 192
EXPERTS = 4
CAP = 32
TOK = 128
NX = 4
NY = 8
C = 512
J = D // C
HALF = C // 2
DHALF = HS // 2
MESH = pl.DeviceIdType.MESH
F32 = jnp.float32
BF16 = jnp.bfloat16


def kernel(
    blocks, gain, w_gate, w_up, w_down, ids, weights, out,
    arrived, picked, rows, wgu, wd, gate_in, up_in, acc, ssq, home_ssq,
    hidden, own_part, pair_out, pair_in, home_out, home_in, out_buf,
    gather_m, combine_hi, combine_lo, zero_w, home_inv,
    load_sem, store_sem, relay_s, relay_r, disp_s, disp_r, pair_s, pair_r,
    gx_s, gx_r, gf_s, gf_r, gd_s, gd_r, dx_s, dx_r, df_s, df_r, dd_s, dd_r,
    back_s, back_r, ret_s, ret_r,
):
    section = lax.axis_index("section")
    sections = lax.axis_size("section")
    place = lax.axis_index("expert")
    core = lax.axis_index("dp")
    y = place // NX
    x = place % NX
    sign = 2 * (y % 2) - 1

    def at_x(step):
        return {"expert": y * NX + (x + step + NX) % NX}

    def at_y(step):
        return {"expert": ((y + step + NY) % NY) * NX + x}

    next_section = {"section": (section + 1) % sections}
    last_section = {"section": (section + sections - 1) % sections}
    other_core = {"dp": 1 - core}
    pair = at_y(-sign)

    def remote(src, dst, send, recv, target):
        return pltpu.make_async_remote_copy(
            src_ref=src, dst_ref=dst, send_sem=send, recv_sem=recv,
            device_id=target, device_id_type=MESH,
        )

    def cols(j):
        return pl.ds(pl.multiple_of(j * C, C), C)

    def load_gate(j):
        return pltpu.make_async_copy(w_gate.at[0, cols(j), :], gate_in.at[j], load_sem.at[0, j])

    def load_up(j):
        return pltpu.make_async_copy(w_up.at[0, cols(j), :], up_in.at[j], load_sem.at[1, j])

    def load_down(j):
        return pltpu.make_async_copy(w_down.at[0, :, cols(j)], wd.at[0, j], load_sem.at[2, j])

    def store_out(j):
        return pltpu.make_async_copy(out_buf.at[j], out.at[0, :, cols(j)], store_sem.at[j])

    def relay(j):
        return remote(blocks.at[0, :, cols(j)], arrived.at[j], relay_s.at[j], relay_r.at[j], next_section)

    def dispatch(d, j):
        step = (sign, -2 * sign, 3 * sign)[d - 1]
        part = pl.ds(d * CAP, CAP)
        return remote(
            picked.at[j, part, :], rows.at[j, part, :], disp_s.at[d - 1, j], disp_r.at[d - 1, j], at_y(step)
        )

    def keep(j):
        return pltpu.make_async_copy(
            picked.at[j, pl.ds(0, CAP), :], rows.at[j, pl.ds(0, CAP), :], load_sem.at[3, j]
        )

    def to_pair(j):
        return remote(
            rows.at[j, pl.ds(0, TOK), :], rows.at[j, pl.ds(TOK, TOK), :], pair_s.at[j], pair_r.at[j], pair
        )

    def ring(buf, count, sx, rx, sf, rf, sd, rd):
        mine = pl.ds(pl.multiple_of(core * count, count), count)

        def own(k, j):
            return remote(
                buf.at[0, j, mine, :], buf.at[(3, 1)[k], j, mine, :], sx.at[k, j], rx.at[k, j], at_x((1, -1)[k])
            )

        def forward(j):
            return remote(
                buf.at[3 - 2 * core, j, mine, :], buf.at[2, j, mine, :], sf.at[j], rf.at[j], at_x(1 - 2 * core)
            )

        def share(s, j):
            here = buf.at[s, j, mine, :]
            return remote(here, here, sd.at[s - 1, j], rd.at[s - 1, j], other_core)

        def share_in(s, j):
            theirs = buf.at[s, j, pl.ds(pl.multiple_of((1 - core) * count, count), count), :]
            return remote(theirs, theirs, sd.at[s - 1, j], rd.at[s - 1, j], other_core)

        return own, forward, share, share_in

    g_own, g_forward, g_share, g_share_in = ring(wgu, HALF, gx_s, gx_r, gf_s, gf_r, gd_s, gd_r)
    d_own, d_forward, d_share, d_share_in = ring(wd, DHALF, dx_s, dx_r, df_s, df_r, dd_s, dd_r)

    def back_to_pair(j):
        return remote(pair_out.at[j], pair_in.at[j], back_s.at[j], back_r.at[j], pair)

    def go_home(d, j):
        part = pl.ds(d * CAP, CAP)
        return remote(
            home_out.at[j, part, :], home_in.at[j, part, :], ret_s.at[d - 1, j], ret_r.at[d - 1, j], at_y(d * sign)
        )

    def keep_home(j):
        return pltpu.make_async_copy(
            home_out.at[j, pl.ds(0, CAP), :], home_in.at[j, pl.ds(0, CAP), :], load_sem.at[4, j]
        )

    def each(fn):
        def body(j, carry):
            fn(j)
            return carry
        lax.fori_loop(0, J, body, 0)

    def staged(length, stages):
        def body(t, carry):
            for lag, fn in stages:
                @pl.when((t >= lag) & (t < lag + J))
                def _(fn=fn, lag=lag):
                    fn(t - lag)
            return carry
        lax.fori_loop(0, length, body, 0)

    def start_loads(j):
        load_gate(j).start()
        load_up(j).start()

    each(start_loads)
    each(lambda j: load_down(j).start())

    barrier = pltpu.get_barrier_semaphore()
    partners = [
        next_section, last_section, other_core, at_x(1), at_x(-1),
        at_y(1), at_y(-1), at_y(2), at_y(-2), at_y(3 * sign),
    ]
    for partner in partners:
        pl.semaphore_signal(barrier, inc=1, device_id=partner, device_id_type=MESH)
    pl.semaphore_wait(barrier, len(partners))

    each(lambda j: relay(j).start())

    def pack(j):
        load_gate(j).wait()
        load_up(j).wait()
        gate = gate_in[j]
        up = up_in[j]
        wgu[0, j, :, 0:128] = gate[:, 0:128]
        wgu[0, j, :, 128:256] = up[:, 0:128]
        wgu[0, j, :, 256:384] = jnp.concatenate([gate[:, 128:192], up[:, 128:192]], axis=1)
        g_own(0, j).start()
        g_own(1, j).start()

    each(pack)

    lane = lax.broadcasted_iota(jnp.int32, (TOK, TOK), 1)
    row = lax.broadcasted_iota(jnp.int32, (TOK, TOK), 0)
    group = lane // CAP
    hop = jnp.where(group == 0, 0, jnp.where(group == 1, sign, jnp.where(group == 2, -2 * sign, 3 * sign)))
    slot_expert = ((y + hop + NY) % NY) // 2
    first = ids[0, :, 0:1] == slot_expert
    second = ids[0, :, 1:2] == slot_expert
    member = jnp.where(first | second, 1.0, 0.0)
    earlier = jnp.where(lane < row, 1.0, 0.0).astype(BF16)
    rank = jnp.dot(earlier, member.astype(BF16), preferred_element_type=F32)
    slot = (lane % CAP).astype(F32)
    table = jnp.where(rank == slot, member, 0.0)
    gather_m[...] = table.T.astype(BF16)
    weighted = table * jnp.where(first, weights[0, :, 0:1], weights[0, :, 1:2])
    high = weighted.astype(BF16)
    combine_hi[...] = high
    combine_lo[...] = (weighted - high.astype(F32)).astype(BF16)
    zero_pick = jnp.where(ids[0] >= EXPERTS, weights[0], 0.0)
    zero_w[...] = jnp.broadcast_to(jnp.sum(zero_pick, axis=1, keepdims=True), (TOK, 128))

    acc[...] = jnp.zeros_like(acc)
    ssq[...] = jnp.zeros_like(ssq)
    home_ssq[...] = jnp.zeros_like(home_ssq)

    def squares(value):
        total = value[:, 0:128] * value[:, 0:128]
        for k in range(1, C // 128):
            piece = value[:, k * 128:(k + 1) * 128]
            total = total + piece * piece
        return total

    def pick_rows(j):
        relay(j).wait_recv()
        block = arrived[j]
        picked[j] = jnp.dot(gather_m[...], block, preferred_element_type=F32).astype(BF16)
        for d in (3, 2, 1):
            dispatch(d, j).start()
        keep(j).start()
        home_ssq[...] += squares(block.astype(F32))

    def pass_weights(j):
        g_own(0, j).wait_recv()
        g_own(1, j).wait_recv()
        g_forward(j).start()
        g_share(3, j).start()
        g_share(1, j).start()

    def pass_rows(j):
        keep(j).wait()
        for d in (1, 2, 3):
            dispatch(d, j).wait_recv()
        to_pair(j).start()

    def share_far(j):
        g_forward(j).wait_recv()
        g_share(2, j).start()

    def first_dots(j):
        to_pair(j).wait_recv()
        for s in (1, 3, 2):
            g_share_in(s, j).wait_recv()
        value = rows[j].astype(F32)
        ssq[...] += squares(value)
        scaled = (value * gain[0:1, cols(j)].astype(F32)).astype(BF16)
        for s in range(NX):
            acc[s] += jnp.dot(scaled, wgu[s, j], preferred_element_type=F32)

    def send_down(j):
        load_down(j).wait()
        d_own(0, j).start()
        d_own(1, j).start()

    staged(
        J + 3,
        [(0, pick_rows), (0, pass_weights), (0, pass_rows), (1, share_far), (3, send_down), (2, first_dots)],
    )

    inverse = lax.rsqrt(jnp.sum(ssq[...], axis=1, keepdims=True) * (1.0 / D) + 1e-06)
    for s in range(NX):
        act = acc[s] * inverse
        gate = act[:, 0:128]
        hidden[s, :, 0:128] = (gate / (1.0 + jnp.exp(-gate)) * act[:, 128:256]).astype(BF16)
        tail = act[:, 256:384]
        tail = tail / (1.0 + jnp.exp(-tail)) * pltpu.roll(tail, 64, 1)
        hidden[s, :, 128:192] = tail[:, 0:64].astype(BF16)
    home_inv[...] = jnp.broadcast_to(
        lax.rsqrt(jnp.sum(home_ssq[...], axis=1, keepdims=True) * (1.0 / D) + 1e-06), (TOK, 128)
    )

    def pass_down(j):
        d_own(0, j).wait_recv()
        d_own(1, j).wait_recv()
        d_forward(j).start()
        d_share(3, j).start()
        d_share(1, j).start()

    def share_down(j):
        d_forward(j).wait_recv()
        d_share(2, j).start()

    def half_dots(begin, j):
        total = jnp.dot(hidden[0, begin:begin + TOK, :], wd[0, j], preferred_element_type=F32)
        for s in range(1, NX):
            total = total + jnp.dot(hidden[s, begin:begin + TOK, :], wd[s, j], preferred_element_type=F32)
        return total

    def second_dots(j):
        for s in (1, 3, 2):
            d_share_in(s, j).wait_recv()
        pair_out[j] = half_dots(TOK, j).astype(BF16)
        back_to_pair(j).start()
        own_part[j] = half_dots(0, j)

    def add_pair(j):
        back_to_pair(j).wait_recv()
        home_out[j] = (own_part[j] + pair_in[j].astype(F32)).astype(BF16)
        for d in (3, 2, 1):
            go_home(d, j).start()
        keep_home(j).start()

    def finish(j):
        keep_home(j).wait()
        for d in (1, 2, 3):
            go_home(d, j).wait_recv()
        value = home_in[j]
        total = jnp.dot(combine_hi[...], value, preferred_element_type=F32)
        total = total + jnp.dot(combine_lo[...], value, preferred_element_type=F32)
        residual = arrived[j].astype(F32)
        normed = (residual * home_inv[:, 0:1] * gain[0:1, cols(j)].astype(F32)).astype(BF16)
        total = residual + zero_w[:, 0:1] * normed.astype(F32) + total
        out_buf[j] = total.astype(BF16)
        store_out(j).start()

    staged(J + 5, [(0, pass_down), (1, share_down), (2, second_dots), (3, add_pair), (5, finish)])

    def drain(j):
        store_out(j).wait()
        relay(j).wait_send()
        for d in (1, 2, 3):
            dispatch(d, j).wait_send()
            go_home(d, j).wait_send()
        to_pair(j).wait_send()
        back_to_pair(j).wait_send()
        for own, forward, share in ((g_own, g_forward, g_share), (d_own, d_forward, d_share)):
            own(0, j).wait_send()
            own(1, j).wait_send()
            forward(j).wait_send()
            for s in (1, 2, 3):
                share(s, j).wait_send()

    each(drain)


def local(blocks, norm_gain, w_gate, w_up, w_down, route_ids, route_weights):
    anywhere = pl.BlockSpec(memory_space=pl.ANY)
    vmem = pl.BlockSpec(memory_space=pltpu.VMEM)
    dma = pltpu.SemaphoreType.DMA
    return pl.pallas_call(
        kernel,
        out_shape=jax.ShapeDtypeStruct(blocks.shape, blocks.dtype),
        in_specs=[anywhere, vmem, anywhere, anywhere, anywhere, vmem, vmem],
        out_specs=anywhere,
        scratch_shapes=[
            pltpu.VMEM((J, TOK, C), BF16),
            pltpu.VMEM((J, TOK, C), BF16),
            pltpu.VMEM((J, 2 * TOK, C), BF16),
            pltpu.VMEM((NX, J, C, 2 * HS), BF16),
            pltpu.VMEM((NX, J, HS, C), BF16),
            pltpu.VMEM((J, C, HS), BF16),
            pltpu.VMEM((J, C, HS), BF16),
            pltpu.VMEM((NX, 2 * TOK, 2 * HS), F32),
            pltpu.VMEM((2 * TOK, 128), F32),
            pltpu.VMEM((TOK, 128), F32),
            pltpu.VMEM((NX, 2 * TOK, HS), BF16),
            pltpu.VMEM((J, TOK, C), F32),
            pltpu.VMEM((J, TOK, C), BF16),
            pltpu.VMEM((J, TOK, C), BF16),
            pltpu.VMEM((J, TOK, C), BF16),
            pltpu.VMEM((J, TOK, C), BF16),
            pltpu.VMEM((J, TOK, C), BF16),
            pltpu.VMEM((TOK, TOK), BF16),
            pltpu.VMEM((TOK, TOK), BF16),
            pltpu.VMEM((TOK, TOK), BF16),
            pltpu.VMEM((TOK, 128), F32),
            pltpu.VMEM((TOK, 128), F32),
            dma((5, J)), dma((J,)),
            dma((J,)), dma((J,)), dma((3, J)), dma((3, J)), dma((J,)), dma((J,)),
            dma((2, J)), dma((2, J)), dma((J,)), dma((J,)), dma((3, J)), dma((3, J)),
            dma((2, J)), dma((2, J)), dma((J,)), dma((J,)), dma((3, J)), dma((3, J)),
            dma((J,)), dma((J,)), dma((3, J)), dma((3, J)),
        ],
        compiler_params=pltpu.CompilerParams(
            collective_id=0, has_side_effects=True, vmem_limit_bytes=50 * 1024 * 1024
        ),
        cost_estimate=pl.CostEstimate(
            flops=2 * 3 * 1024 * D * HS, bytes_accessed=6 * 1024 * 1024, transcendentals=256 * 768
        ),
    )(blocks, norm_gain, w_gate, w_up, w_down, route_ids, route_weights)


def solution(mesh):
    placed = (
        P("section", ("dp", "expert"), None),
        P("section", None),
        P("section", None, "expert"),
        P("section", None, "expert"),
        P("section", "expert", None),
        P("section", ("dp", "expert"), None),
        P("section", ("dp", "expert"), None),
    )
    return jax.shard_map(
        local,
        mesh=mesh,
        in_specs=placed,
        out_specs=P("section", ("dp", "expert"), None),
        check_vma=False,
    )
```

```python
import jax
import jax.numpy as jnp
from jax import lax
from jax.experimental import pallas as pl
from jax.experimental.pallas import tpu as pltpu
from jax.sharding import PartitionSpec as P

D = 3072
HS = 192
EXPERTS = 4
CAP = 32
TOK = 128
NX = 4
NY = 8
C = 512
J = D // C
DHALF = HS // 2
MESH = pl.DeviceIdType.MESH
F32 = jnp.float32
BF16 = jnp.bfloat16


def kernel(
    blocks, gain, w_gate, w_up, w_down, ids, weights, out,
    arrived, picked, rows, wgu, wd, acc, ssq, home_ssq,
    hidden, own_part, pair_out, pair_in, home_out, home_in, out_buf,
    gather_m, combine_hi, combine_lo, zero_w, home_inv,
    load_sem, store_sem, relay_s, relay_r, disp_s, disp_r, pair_s, pair_r,
    gx_s, gx_r, gf_s, gf_r, gd_s, gd_r, dx_s, dx_r, df_s, df_r, dd_s, dd_r,
    back_s, back_r, ret_s, ret_r,
):
    section = lax.axis_index("section")
    sections = lax.axis_size("section")
    place = lax.axis_index("expert")
    core = lax.axis_index("dp")
    y = place // NX
    x = place % NX
    sign = 2 * (y % 2) - 1

    def at_x(step):
        return {"expert": y * NX + (x + step + NX) % NX}

    def at_y(step):
        return {"expert": ((y + step + NY) % NY) * NX + x}

    next_section = {"section": (section + 1) % sections}
    last_section = {"section": (section + sections - 1) % sections}
    other_core = {"dp": 1 - core}
    pair = at_y(-sign)

    def remote(src, dst, send, recv, target):
        return pltpu.make_async_remote_copy(
            src_ref=src, dst_ref=dst, send_sem=send, recv_sem=recv,
            device_id=target, device_id_type=MESH,
        )

    def cols(j):
        return pl.ds(pl.multiple_of(j * C, C), C)

    def load_gate(j):
        return pltpu.make_async_copy(w_gate.at[0, :, cols(j)], wgu.at[j, 0, pl.ds(0, HS), :], load_sem.at[0, j])

    def load_up(j):
        return pltpu.make_async_copy(w_up.at[0, :, cols(j)], wgu.at[j, 0, pl.ds(HS, HS), :], load_sem.at[1, j])

    def load_down(j):
        return pltpu.make_async_copy(w_down.at[0, :, cols(j)], wd.at[j, 0], load_sem.at[2, j])

    def store_out(j):
        return pltpu.make_async_copy(out_buf.at[j], out.at[0, :, cols(j)], store_sem.at[j])

    def relay(j):
        return remote(blocks.at[0, :, cols(j)], arrived.at[j], relay_s.at[j], relay_r.at[j], next_section)

    def dispatch(d, j):
        step = (sign, -2 * sign, 3 * sign)[d - 1]
        part = pl.ds(d * CAP, CAP)
        return remote(
            picked.at[j, part, :], rows.at[j, part, :], disp_s.at[d - 1, j], disp_r.at[d - 1, j], at_y(step)
        )

    def keep(j):
        return pltpu.make_async_copy(
            picked.at[j, pl.ds(0, CAP), :], rows.at[j, pl.ds(0, CAP), :], load_sem.at[3, j]
        )

    def to_pair(j):
        return remote(
            rows.at[j, pl.ds(0, TOK), :], rows.at[j, pl.ds(TOK, TOK), :], pair_s.at[j], pair_r.at[j], pair
        )

    def ring(buf, count, sx, rx, sf, rf, sd, rd):
        mine = pl.ds(pl.multiple_of(core * count, count), count)

        def own(k, j):
            return remote(
                buf.at[j, 0, mine, :], buf.at[j, (3, 1)[k], mine, :], sx.at[k, j], rx.at[k, j], at_x((1, -1)[k])
            )

        def forward(j):
            return remote(
                buf.at[j, 3 - 2 * core, mine, :], buf.at[j, 2, mine, :], sf.at[j], rf.at[j], at_x(1 - 2 * core)
            )

        def share(s, j):
            here = buf.at[j, s, mine, :]
            return remote(here, here, sd.at[s - 1, j], rd.at[s - 1, j], other_core)

        def share_in(s, j):
            theirs = buf.at[j, s, pl.ds(pl.multiple_of((1 - core) * count, count), count), :]
            return remote(theirs, theirs, sd.at[s - 1, j], rd.at[s - 1, j], other_core)

        return own, forward, share, share_in

    g_own, g_forward, g_share, g_share_in = ring(wgu, HS, gx_s, gx_r, gf_s, gf_r, gd_s, gd_r)
    d_own, d_forward, d_share, d_share_in = ring(wd, DHALF, dx_s, dx_r, df_s, df_r, dd_s, dd_r)

    def back_to_pair(j):
        return remote(pair_out.at[j], pair_in.at[j], back_s.at[j], back_r.at[j], pair)

    def go_home(d, j):
        part = pl.ds(d * CAP, CAP)
        return remote(
            home_out.at[j, part, :], home_in.at[j, part, :], ret_s.at[d - 1, j], ret_r.at[d - 1, j], at_y(d * sign)
        )

    def keep_home(j):
        return pltpu.make_async_copy(
            home_out.at[j, pl.ds(0, CAP), :], home_in.at[j, pl.ds(0, CAP), :], load_sem.at[4, j]
        )

    def each(fn):
        def body(j, carry):
            fn(j)
            return carry
        lax.fori_loop(0, J, body, 0)

    def staged(length, stages):
        def body(t, carry):
            for lag, fn in stages:
                @pl.when((t >= lag) & (t < lag + J))
                def _(fn=fn, lag=lag):
                    fn(t - lag)
            return carry
        lax.fori_loop(0, length, body, 0)

    def start_loads(j):
        load_gate(j).start()
        load_up(j).start()

    each(start_loads)
    each(lambda j: load_down(j).start())

    barrier = pltpu.get_barrier_semaphore()
    partners = [
        next_section, last_section, other_core, at_x(1), at_x(-1),
        at_y(1), at_y(-1), at_y(2), at_y(-2), at_y(3 * sign),
    ]
    for partner in partners:
        pl.semaphore_signal(barrier, inc=1, device_id=partner, device_id_type=MESH)
    pl.semaphore_wait(barrier, len(partners))

    each(lambda j: relay(j).start())

    def send_first(j):
        load_gate(j).wait()
        load_up(j).wait()
        g_own(0, j).start()
        g_own(1, j).start()

    each(send_first)

    lane = lax.broadcasted_iota(jnp.int32, (TOK, TOK), 1)
    row = lax.broadcasted_iota(jnp.int32, (TOK, TOK), 0)
    group = row // CAP
    hop = jnp.where(group == 0, 0, jnp.where(group == 1, sign, jnp.where(group == 2, -2 * sign, 3 * sign)))
    slot_expert = ((y + hop + NY) % NY) // 2
    first = ids[0, 0:1, :] == slot_expert
    second = ids[0, 1:2, :] == slot_expert
    member = jnp.where(first | second, 1.0, 0.0)
    earlier = jnp.where(row < lane, 1.0, 0.0).astype(BF16)
    rank = jnp.dot(member.astype(BF16), earlier, preferred_element_type=F32)
    slot = (row % CAP).astype(F32)
    table = jnp.where(rank == slot, member, 0.0)
    gather_m[...] = table.astype(BF16)
    weighted = (table * jnp.where(first, weights[0, 0:1, :], weights[0, 1:2, :])).T
    high = weighted.astype(BF16)
    combine_hi[...] = high
    combine_lo[...] = (weighted - high.astype(F32)).astype(BF16)
    zero_pick = jnp.where(ids[0] >= EXPERTS, weights[0], 0.0)
    zero_sum = jnp.sum(zero_pick, axis=0, keepdims=True)
    zero_w[...] = jnp.broadcast_to(zero_sum, (TOK, TOK)).T

    acc[...] = jnp.zeros_like(acc)
    ssq[...] = jnp.zeros_like(ssq)
    home_ssq[...] = jnp.zeros_like(home_ssq)

    def squares(value):
        total = value[:, 0:128] * value[:, 0:128]
        for k in range(1, C // 128):
            piece = value[:, k * 128:(k + 1) * 128]
            total = total + piece * piece
        return total

    def pick_rows(j):
        relay(j).wait_recv()
        block = arrived[j]
        picked[j] = jnp.dot(gather_m[...], block, preferred_element_type=F32).astype(BF16)
        for d in (3, 2, 1):
            dispatch(d, j).start()
        keep(j).start()
        home_ssq[...] += squares(block.astype(F32))

    def pass_weights(j):
        g_own(0, j).wait_recv()
        g_own(1, j).wait_recv()
        g_forward(j).start()
        g_share(3, j).start()
        g_share(1, j).start()

    def pass_rows(j):
        keep(j).wait()
        for d in (1, 2, 3):
            dispatch(d, j).wait_recv()
        to_pair(j).start()

    def share_far(j):
        g_forward(j).wait_recv()
        g_share(2, j).start()

    def first_dots(j):
        to_pair(j).wait_recv()
        for s in (1, 3, 2):
            g_share_in(s, j).wait_recv()
        value = rows[j].astype(F32)
        ssq[...] += squares(value)
        scaled = (value * gain[0:1, cols(j)].astype(F32)).astype(BF16)
        acc[...] += lax.dot_general(
            scaled, wgu[j].reshape(NX * 2 * HS, C), (((1,), (1,)), ((), ())), preferred_element_type=F32
        )

    def send_down(j):
        load_down(j).wait()
        d_own(0, j).start()
        d_own(1, j).start()

    staged(
        J + 3,
        [(0, pick_rows), (0, pass_weights), (0, pass_rows), (1, share_far), (3, send_down), (2, first_dots)],
    )

    inverse = lax.rsqrt(jnp.sum(ssq[...], axis=1, keepdims=True) * (1.0 / D) + 1e-06)
    low = lax.broadcasted_iota(jnp.int32, (2 * TOK, 128), 1) < 64
    for s in range(NX):
        base = s * 2 * HS
        gate = acc[:, base:base + 128] * inverse
        mid = acc[:, base + 128:base + 256] * inverse
        up = pltpu.roll(acc[:, base + 256:base + 384] * inverse, 64, 1)
        hidden[s, :, 0:128] = (gate / (1.0 + jnp.exp(-gate)) * jnp.where(low, pltpu.roll(mid, 64, 1), up)).astype(BF16)
        hidden[s, :, 128:192] = (mid / (1.0 + jnp.exp(-mid)) * up)[:, 0:64].astype(BF16)
    home_inv[...] = jnp.broadcast_to(
        lax.rsqrt(jnp.sum(home_ssq[...], axis=1, keepdims=True) * (1.0 / D) + 1e-06), (TOK, 128)
    )

    def pass_down(j):
        d_own(0, j).wait_recv()
        d_own(1, j).wait_recv()
        d_forward(j).start()
        d_share(3, j).start()
        d_share(1, j).start()

    def share_down(j):
        d_forward(j).wait_recv()
        d_share(2, j).start()

    def half_dots(begin, j):
        total = jnp.dot(hidden[0, begin:begin + TOK, :], wd[j, 0], preferred_element_type=F32)
        for s in range(1, NX):
            total = total + jnp.dot(hidden[s, begin:begin + TOK, :], wd[j, s], preferred_element_type=F32)
        return total

    def second_dots(j):
        for s in (1, 3, 2):
            d_share_in(s, j).wait_recv()
        pair_out[j] = half_dots(TOK, j).astype(BF16)
        back_to_pair(j).start()
        own_part[j] = half_dots(0, j)

    def add_pair(j):
        back_to_pair(j).wait_recv()
        home_out[j] = (own_part[j] + pair_in[j].astype(F32)).astype(BF16)
        for d in (3, 2, 1):
            go_home(d, j).start()
        keep_home(j).start()

    def finish(j):
        keep_home(j).wait()
        for d in (1, 2, 3):
            go_home(d, j).wait_recv()
        value = home_in[j]
        total = jnp.dot(combine_hi[...], value, preferred_element_type=F32)
        total = total + jnp.dot(combine_lo[...], value, preferred_element_type=F32)
        residual = arrived[j].astype(F32)
        normed = (residual * home_inv[:, 0:1] * gain[0:1, cols(j)].astype(F32)).astype(BF16)
        total = residual + zero_w[:, 0:1] * normed.astype(F32) + total
        out_buf[j] = total.astype(BF16)
        store_out(j).start()

    staged(J + 5, [(0, pass_down), (1, share_down), (2, second_dots), (3, add_pair), (5, finish)])

    def drain(j):
        store_out(j).wait()
        relay(j).wait_send()
        for d in (1, 2, 3):
            dispatch(d, j).wait_send()
            go_home(d, j).wait_send()
        to_pair(j).wait_send()
        back_to_pair(j).wait_send()
        for own, forward, share in ((g_own, g_forward, g_share), (d_own, d_forward, d_share)):
            own(0, j).wait_send()
            own(1, j).wait_send()
            forward(j).wait_send()
            for s in (1, 2, 3):
                share(s, j).wait_send()

    each(drain)


def local(blocks, norm_gain, w_gate, w_up, w_down, route_ids, route_weights):
    anywhere = pl.BlockSpec(memory_space=pl.ANY)
    vmem = pl.BlockSpec(memory_space=pltpu.VMEM)
    dma = pltpu.SemaphoreType.DMA
    return pl.pallas_call(
        kernel,
        out_shape=jax.ShapeDtypeStruct(blocks.shape, blocks.dtype),
        in_specs=[anywhere, vmem, anywhere, anywhere, anywhere, vmem, vmem],
        out_specs=anywhere,
        scratch_shapes=[
            pltpu.VMEM((J, TOK, C), BF16),
            pltpu.VMEM((J, TOK, C), BF16),
            pltpu.VMEM((J, 2 * TOK, C), BF16),
            pltpu.VMEM((J, NX, 2 * HS, C), BF16),
            pltpu.VMEM((J, NX, HS, C), BF16),
            pltpu.VMEM((2 * TOK, NX * 2 * HS), F32),
            pltpu.VMEM((2 * TOK, 128), F32),
            pltpu.VMEM((TOK, 128), F32),
            pltpu.VMEM((NX, 2 * TOK, HS), BF16),
            pltpu.VMEM((J, TOK, C), F32),
            pltpu.VMEM((J, TOK, C), BF16),
            pltpu.VMEM((J, TOK, C), BF16),
            pltpu.VMEM((J, TOK, C), BF16),
            pltpu.VMEM((J, TOK, C), BF16),
            pltpu.VMEM((J, TOK, C), BF16),
            pltpu.VMEM((TOK, TOK), BF16),
            pltpu.VMEM((TOK, TOK), BF16),
            pltpu.VMEM((TOK, TOK), BF16),
            pltpu.VMEM((TOK, 128), F32),
            pltpu.VMEM((TOK, 128), F32),
            dma((5, J)), dma((J,)),
            dma((J,)), dma((J,)), dma((3, J)), dma((3, J)), dma((J,)), dma((J,)),
            dma((2, J)), dma((2, J)), dma((J,)), dma((J,)), dma((3, J)), dma((3, J)),
            dma((2, J)), dma((2, J)), dma((J,)), dma((J,)), dma((3, J)), dma((3, J)),
            dma((J,)), dma((J,)), dma((3, J)), dma((3, J)),
        ],
        compiler_params=pltpu.CompilerParams(
            collective_id=0, has_side_effects=True, vmem_limit_bytes=50 * 1024 * 1024
        ),
        cost_estimate=pl.CostEstimate(
            flops=2 * 3 * 1024 * D * HS, bytes_accessed=6 * 1024 * 1024, transcendentals=256 * 768
        ),
    )(
        blocks, norm_gain, jnp.swapaxes(w_gate, 1, 2), jnp.swapaxes(w_up, 1, 2), w_down,
        jnp.swapaxes(route_ids, 1, 2), jnp.swapaxes(route_weights, 1, 2),
    )


def solution(mesh):
    placed = (
        P("section", ("dp", "expert"), None),
        P("section", None),
        P("section", None, "expert"),
        P("section", None, "expert"),
        P("section", "expert", None),
        P("section", ("dp", "expert"), None),
        P("section", ("dp", "expert"), None),
    )
    return jax.shard_map(
        local,
        mesh=mesh,
        in_specs=placed,
        out_specs=P("section", ("dp", "expert"), None),
        check_vma=False,
    )
```

```python
import jax
import jax.numpy as jnp
from jax import lax
from jax.experimental import pallas as pl
from jax.experimental.pallas import tpu as pltpu
from jax.sharding import PartitionSpec as P

D = 3072
HS = 192
EXPERTS = 4
CAP = 32
TOK = 128
NX = 4
NY = 8
C = 512
J = D // C
DHALF = HS // 2
NEAR = 3 * 2 * HS
MESH = pl.DeviceIdType.MESH
F32 = jnp.float32
BF16 = jnp.bfloat16


def kernel(
    blocks, gain_in, w_gate, w_up, w_down, ids_in, weights_in, out,
    gain, ids, weights, arrived, picked, rows, wgu, wd, scaled, acc, ssq, home_ssq,
    hidden, own_part, pair_out, pair_in, home_out, home_in, out_buf,
    gather_m, combine_hi, combine_lo, zero_w, home_inv,
    small_sem, load_sem, store_sem, relay_s, relay_r, disp_s, disp_r, pair_s, pair_r,
    gx_s, gx_r, gf_s, gf_r, gd_s, gd_r, dx_s, dx_r, df_s, df_r, dd_s, dd_r,
    back_s, back_r, ret_s, ret_r,
):
    section = lax.axis_index("section")
    sections = lax.axis_size("section")
    place = lax.axis_index("expert")
    core = lax.axis_index("dp")
    y = place // NX
    x = place % NX
    sign = 2 * (y % 2) - 1

    def at_x(step):
        return {"expert": y * NX + (x + step + NX) % NX}

    def at_y(step):
        return {"expert": ((y + step + NY) % NY) * NX + x}

    next_section = {"section": (section + 1) % sections}
    last_section = {"section": (section + sections - 1) % sections}
    other_core = {"dp": 1 - core}
    pair = at_y(-sign)

    def remote(src, dst, send, recv, target):
        return pltpu.make_async_remote_copy(
            src_ref=src, dst_ref=dst, send_sem=send, recv_sem=recv,
            device_id=target, device_id_type=MESH,
        )

    def cols(j):
        return pl.ds(pl.multiple_of(j * C, C), C)

    def load_gate(j):
        return pltpu.make_async_copy(w_gate.at[0, :, cols(j)], wgu.at[j, 0, pl.ds(0, HS), :], load_sem.at[0, j])

    def load_up(j):
        return pltpu.make_async_copy(w_up.at[0, :, cols(j)], wgu.at[j, 0, pl.ds(HS, HS), :], load_sem.at[1, j])

    def load_down(j):
        return pltpu.make_async_copy(w_down.at[0, :, cols(j)], wd.at[j, 0], load_sem.at[2, j])

    def store_out(j):
        return pltpu.make_async_copy(out_buf.at[j], out.at[0, :, cols(j)], store_sem.at[j])

    def relay(j):
        return remote(blocks.at[0, :, cols(j)], arrived.at[j], relay_s.at[j], relay_r.at[j], next_section)

    def dispatch(d, j):
        step = (sign, -2 * sign, 3 * sign)[d - 1]
        part = pl.ds(d * CAP, CAP)
        return remote(
            picked.at[j, part, :], rows.at[j, part, :], disp_s.at[d - 1, j], disp_r.at[d - 1, j], at_y(step)
        )

    def keep(j):
        return pltpu.make_async_copy(
            picked.at[j, pl.ds(0, CAP), :], rows.at[j, pl.ds(0, CAP), :], load_sem.at[3, j]
        )

    def to_pair(j):
        return remote(
            rows.at[j, pl.ds(0, TOK), :], rows.at[j, pl.ds(TOK, TOK), :], pair_s.at[j], pair_r.at[j], pair
        )

    def ring(buf, count, sx, rx, sf, rf, sd, rd):
        mine = pl.ds(pl.multiple_of(core * count, count), count)

        def own(k, j):
            return remote(
                buf.at[j, 0, mine, :], buf.at[j, 2 - k, mine, :], sx.at[k, j], rx.at[k, j], at_x((1, -1)[k])
            )

        def forward(j):
            return remote(
                buf.at[j, 2 - core, mine, :], buf.at[j, 3, mine, :], sf.at[j], rf.at[j], at_x(1 - 2 * core)
            )

        def share(s, j):
            here = buf.at[j, s, mine, :]
            return remote(here, here, sd.at[s - 1, j], rd.at[s - 1, j], other_core)

        def share_in(s, j):
            theirs = buf.at[j, s, pl.ds(pl.multiple_of((1 - core) * count, count), count), :]
            return remote(theirs, theirs, sd.at[s - 1, j], rd.at[s - 1, j], other_core)

        return own, forward, share, share_in

    g_own, g_forward, g_share, g_share_in = ring(wgu, HS, gx_s, gx_r, gf_s, gf_r, gd_s, gd_r)
    d_own, d_forward, d_share, d_share_in = ring(wd, DHALF, dx_s, dx_r, df_s, df_r, dd_s, dd_r)

    def back_to_pair(j):
        return remote(pair_out.at[j], pair_in.at[j], back_s.at[j], back_r.at[j], pair)

    def go_home(d, j):
        part = pl.ds(d * CAP, CAP)
        return remote(
            home_out.at[j, part, :], home_in.at[j, part, :], ret_s.at[d - 1, j], ret_r.at[d - 1, j], at_y(d * sign)
        )

    def keep_home(j):
        return pltpu.make_async_copy(
            home_out.at[j, pl.ds(0, CAP), :], home_in.at[j, pl.ds(0, CAP), :], load_sem.at[4, j]
        )

    def each(fn):
        def body(j, carry):
            fn(j)
            return carry
        lax.fori_loop(0, J, body, 0)

    def staged(steps, stages):
        def body(t, carry):
            for lag, first, fn in stages:
                @pl.when((t >= lag + first) & (t < lag + J))
                def _(fn=fn, lag=lag):
                    fn(t - lag)
            return carry
        lax.fori_loop(0, steps, body, 0)

    def start_loads(j):
        load_gate(j).start()
        load_up(j).start()

    small = [
        pltpu.make_async_copy(src, dst, small_sem.at[k])
        for k, (src, dst) in enumerate(((ids_in.at[0], ids), (weights_in.at[0], weights), (gain_in, gain)))
    ]
    for copy in small:
        copy.start()
    each(start_loads)
    each(lambda j: load_down(j).start())

    barrier = pltpu.get_barrier_semaphore()
    partners = [
        next_section, last_section, other_core, at_x(1), at_x(-1),
        at_y(1), at_y(-1), at_y(2), at_y(-2), at_y(3 * sign),
    ]
    for partner in partners:
        pl.semaphore_signal(barrier, inc=1, device_id=partner, device_id_type=MESH)
    for copy in small:
        copy.wait()
    lane = lax.broadcasted_iota(jnp.int32, (TOK, TOK), 1)
    row = lax.broadcasted_iota(jnp.int32, (TOK, TOK), 0)
    group = row // CAP
    hop = jnp.where(group == 0, 0, jnp.where(group == 1, sign, jnp.where(group == 2, -2 * sign, 3 * sign)))
    slot_expert = ((y + hop + NY) % NY) // 2
    first = ids[0:1, :] == slot_expert
    second = ids[1:2, :] == slot_expert
    member = jnp.where(first | second, 1.0, 0.0)
    earlier = jnp.where(row < lane, 1.0, 0.0).astype(BF16)
    rank = jnp.dot(member.astype(BF16), earlier, preferred_element_type=F32)
    slot = (row % CAP).astype(F32)
    table = jnp.where(rank == slot, member, 0.0)
    gather_m[...] = table.astype(BF16)
    weighted = (table * jnp.where(first, weights[0:1, :], weights[1:2, :])).T
    high = weighted.astype(BF16)
    combine_hi[...] = high
    combine_lo[...] = (weighted - high.astype(F32)).astype(BF16)
    zero_pick = jnp.where(ids[...] >= EXPERTS, weights[...], 0.0)
    zero_sum = jnp.sum(zero_pick, axis=0, keepdims=True)
    zero_w[...] = jnp.broadcast_to(zero_sum, (TOK, TOK)).T

    acc[...] = jnp.zeros_like(acc)
    ssq[...] = jnp.zeros_like(ssq)
    home_ssq[...] = jnp.zeros_like(home_ssq)

    pl.semaphore_wait(barrier, len(partners))

    each(lambda j: relay(j).start())

    def send_first(j):
        load_gate(j).wait()
        load_up(j).wait()
        g_own(0, j).start()
        g_own(1, j).start()

    each(send_first)

    def squares(value):
        total = value[:, 0:128] * value[:, 0:128]
        for k in range(1, C // 128):
            piece = value[:, k * 128:(k + 1) * 128]
            total = total + piece * piece
        return total

    def pick_rows(j):
        relay(j).wait_recv()
        block = arrived[j]
        picked[j] = jnp.dot(gather_m[...], block, preferred_element_type=F32).astype(BF16)
        for d in (3, 2, 1):
            dispatch(d, j).start()
        keep(j).start()
        home_ssq[...] += squares(block.astype(F32))

    def pass_weights(j):
        g_own(0, j).wait_recv()
        g_own(1, j).wait_recv()
        g_forward(j).start()
        g_share(1, j).start()
        g_share(2, j).start()

    def pass_rows(j):
        keep(j).wait()
        for d in (1, 2, 3):
            dispatch(d, j).wait_recv()
        to_pair(j).start()

    def share_far(j):
        g_forward(j).wait_recv()
        g_share(3, j).start()

    def near_dots(j):
        to_pair(j).wait_recv()
        value = rows[j].astype(F32)
        ssq[...] += squares(value)
        scaled[j] = (value * gain[0:1, cols(j)].astype(F32)).astype(BF16)
        for s in (1, 2):
            g_share_in(s, j).wait_recv()
        acc[:, 0:NEAR] += lax.dot_general(
            scaled[j], wgu[j, 0:3].reshape(NEAR, C), (((1,), (1,)), ((), ())), preferred_element_type=F32
        )

    def far_dots(j):
        g_share_in(3, j).wait_recv()
        acc[:, NEAR:] += lax.dot_general(
            scaled[j], wgu[j, 3], (((1,), (1,)), ((), ())), preferred_element_type=F32
        )

    def send_down(j):
        load_down(j).wait()
        d_own(0, j).start()
        d_own(1, j).start()

    def pass_down(j):
        d_own(0, j).wait_recv()
        d_own(1, j).wait_recv()
        d_forward(j).start()
        d_share(1, j).start()
        d_share(2, j).start()

    def share_down(j):
        d_forward(j).wait_recv()
        d_share(3, j).start()

    def activate(slots):
        inverse = lax.rsqrt(jnp.sum(ssq[...], axis=1, keepdims=True) * (1.0 / D) + 1e-06)
        low = lax.broadcasted_iota(jnp.int32, (2 * TOK, 128), 1) < 64
        for s in slots:
            base = s * 2 * HS
            gate = acc[:, base:base + 128] * inverse
            mid = acc[:, base + 128:base + 256] * inverse
            up = pltpu.roll(acc[:, base + 256:base + 384] * inverse, 64, 1)
            other = jnp.where(low, pltpu.roll(mid, 64, 1), up)
            hidden[s, :, 0:128] = (gate / (1.0 + jnp.exp(-gate)) * other).astype(BF16)
            hidden[s, :, 128:192] = (mid / (1.0 + jnp.exp(-mid)) * up)[:, 0:64].astype(BF16)

    def activate_near(j):
        activate(range(3))
        home_inv[...] = jnp.broadcast_to(
            lax.rsqrt(jnp.sum(home_ssq[...], axis=1, keepdims=True) * (1.0 / D) + 1e-06), (TOK, 128)
        )

    staged(J, [(0, 0, pick_rows), (1, 0, pass_rows), (0, 0, pass_weights), (2, 0, near_dots)])
    pass_rows(J - 1)
    send_down(0)
    send_down(1)
    staged(
        J,
        [(0, 0, share_far), (3 - J, J - 2, near_dots), (1, 0, far_dots), (4 - J, J - 1, activate_near)],
    )
    pass_down(0)
    send_down(2)
    far_dots(J - 1)
    activate((3,))

    def half_dots(begin, j):
        total = jnp.dot(hidden[0, begin:begin + TOK, :], wd[j, 0], preferred_element_type=F32)
        for s in range(1, NX):
            total = total + jnp.dot(hidden[s, begin:begin + TOK, :], wd[j, s], preferred_element_type=F32)
        return total

    def second_dots(j):
        for s in (1, 2, 3):
            d_share_in(s, j).wait_recv()
        pair_out[j] = half_dots(TOK, j).astype(BF16)
        back_to_pair(j).start()
        own_part[j] = half_dots(0, j)

    def add_pair(j):
        back_to_pair(j).wait_recv()
        home_out[j] = (own_part[j] + pair_in[j].astype(F32)).astype(BF16)
        for d in (3, 2, 1):
            go_home(d, j).start()
        keep_home(j).start()

    def finish(j):
        keep_home(j).wait()
        for d in (1, 2, 3):
            go_home(d, j).wait_recv()
        value = home_in[j]
        total = jnp.dot(combine_hi[...], value, preferred_element_type=F32)
        total = total + jnp.dot(combine_lo[...], value, preferred_element_type=F32)
        residual = arrived[j].astype(F32)
        normed = (residual * home_inv[:, 0:1] * gain[0:1, cols(j)].astype(F32)).astype(BF16)
        total = residual + zero_w[:, 0:1] * normed.astype(F32) + total
        out_buf[j] = total.astype(BF16)
        store_out(j).start()

    pass_down(1)
    send_down(3)
    share_down(0)
    staged(
        J + 3,
        [
            (0, 0, second_dots), (-2, 2, pass_down), (-4, 4, send_down), (-1, 1, share_down),
            (1, 0, add_pair), (3, 0, finish),
        ],
    )

    def drain(j):
        store_out(j).wait()
        relay(j).wait_send()
        for d in (1, 2, 3):
            dispatch(d, j).wait_send()
            go_home(d, j).wait_send()
        to_pair(j).wait_send()
        back_to_pair(j).wait_send()
        for own, forward, share in ((g_own, g_forward, g_share), (d_own, d_forward, d_share)):
            own(0, j).wait_send()
            own(1, j).wait_send()
            forward(j).wait_send()
            for s in (1, 2, 3):
                share(s, j).wait_send()

    each(drain)


def local(blocks, norm_gain, w_gate, w_up, w_down, route_ids, route_weights):
    anywhere = pl.BlockSpec(memory_space=pl.ANY)
    dma = pltpu.SemaphoreType.DMA
    return pl.pallas_call(
        kernel,
        out_shape=jax.ShapeDtypeStruct(blocks.shape, blocks.dtype),
        in_specs=[anywhere] * 7,
        out_specs=anywhere,
        scratch_shapes=[
            pltpu.VMEM((1, D), BF16),
            pltpu.VMEM((2, TOK), jnp.int32),
            pltpu.VMEM((2, TOK), F32),
            pltpu.VMEM((J, TOK, C), BF16),
            pltpu.VMEM((J, TOK, C), BF16),
            pltpu.VMEM((J, 2 * TOK, C), BF16),
            pltpu.VMEM((J, NX, 2 * HS, C), BF16),
            pltpu.VMEM((J, NX, HS, C), BF16),
            pltpu.VMEM((J, 2 * TOK, C), BF16),
            pltpu.VMEM((2 * TOK, NX * 2 * HS), F32),
            pltpu.VMEM((2 * TOK, 128), F32),
            pltpu.VMEM((TOK, 128), F32),
            pltpu.VMEM((NX, 2 * TOK, HS), BF16),
            pltpu.VMEM((J, TOK, C), F32),
            pltpu.VMEM((J, TOK, C), BF16),
            pltpu.VMEM((J, TOK, C), BF16),
            pltpu.VMEM((J, TOK, C), BF16),
            pltpu.VMEM((J, TOK, C), BF16),
            pltpu.VMEM((J, TOK, C), BF16),
            pltpu.VMEM((TOK, TOK), BF16),
            pltpu.VMEM((TOK, TOK), BF16),
            pltpu.VMEM((TOK, TOK), BF16),
            pltpu.VMEM((TOK, 128), F32),
            pltpu.VMEM((TOK, 128), F32),
            dma((3,)), dma((5, J)), dma((J,)),
            dma((J,)), dma((J,)), dma((3, J)), dma((3, J)), dma((J,)), dma((J,)),
            dma((2, J)), dma((2, J)), dma((J,)), dma((J,)), dma((3, J)), dma((3, J)),
            dma((2, J)), dma((2, J)), dma((J,)), dma((J,)), dma((3, J)), dma((3, J)),
            dma((J,)), dma((J,)), dma((3, J)), dma((3, J)),
        ],
        compiler_params=pltpu.CompilerParams(
            collective_id=0, has_side_effects=True, vmem_limit_bytes=60 * 1024 * 1024
        ),
        cost_estimate=pl.CostEstimate(
            flops=2 * 3 * 1024 * D * HS, bytes_accessed=6 * 1024 * 1024, transcendentals=256 * 768
        ),
    )(
        blocks, norm_gain, jnp.swapaxes(w_gate, 1, 2), jnp.swapaxes(w_up, 1, 2), w_down,
        jnp.swapaxes(route_ids, 1, 2), jnp.swapaxes(route_weights, 1, 2),
    )


def solution(mesh):
    placed = (
        P("section", ("dp", "expert"), None),
        P("section", None),
        P("section", None, "expert"),
        P("section", None, "expert"),
        P("section", "expert", None),
        P("section", ("dp", "expert"), None),
        P("section", ("dp", "expert"), None),
    )
    return jax.shard_map(
        local,
        mesh=mesh,
        in_specs=placed,
        out_specs=P("section", ("dp", "expert"), None),
        check_vma=False,
    )
```

```python
import jax
import jax.numpy as jnp
from jax import lax
from jax.experimental import pallas as pl
from jax.experimental.pallas import tpu as pltpu
from jax.sharding import PartitionSpec as P

D = 3072
HS = 192
EXPERTS = 4
CAP = 32
TOK = 128
NX = 4
NY = 8
C = 512
J = D // C
C2 = 256
WIDE = D // 2
J2 = WIDE // C2
NEAR = 3 * 2 * HS
MESH = pl.DeviceIdType.MESH
F32 = jnp.float32
BF16 = jnp.bfloat16


def kernel(
    blocks, gain_in, w_gate, w_up, w_down, ids_in, weights_in, out,
    gain, ids, weights, arrived, picked, rows, wgu, wd, scaled, acc, ssq, home_ssq,
    hidden, pair_hidden, packed_out, packed_in, tail_two, home_out, home_in, out_buf,
    gather_m, combine_hi, combine_lo, zero_w, home_inv,
    small_sem, load_sem, down_sem, store_sem, relay_s, relay_r, disp_s, disp_r, pair_s, pair_r,
    gx_s, gx_r, gf_s, gf_r, gd_s, gd_r, dx_s, dx_r, df_s, df_r, dd_s, dd_r,
    pd_s, pd_r, pc_s, pc_r, act_s, act_r, ret_s, ret_r,
):
    section = lax.axis_index("section")
    sections = lax.axis_size("section")
    place = lax.axis_index("expert")
    core = lax.axis_index("dp")
    y = place // NX
    x = place % NX
    sign = 2 * (y % 2) - 1

    def at_x(step):
        return {"expert": y * NX + (x + step + NX) % NX}

    def at_y(step):
        return {"expert": ((y + step + NY) % NY) * NX + x}

    next_section = {"section": (section + 1) % sections}
    last_section = {"section": (section + sections - 1) % sections}
    other_core = {"dp": 1 - core}
    pair = at_y(-sign)
    half = y % 2

    def remote(src, dst, send, recv, target):
        return pltpu.make_async_remote_copy(
            src_ref=src, dst_ref=dst, send_sem=send, recv_sem=recv,
            device_id=target, device_id_type=MESH,
        )

    def cols(j):
        return pl.ds(pl.multiple_of(j * C, C), C)

    def cols2(side, j):
        return pl.ds(pl.multiple_of(side * WIDE + j * C2, C2), C2)

    def load_gate(j):
        return pltpu.make_async_copy(w_gate.at[0, :, cols(j)], wgu.at[j, 0, pl.ds(0, HS), :], load_sem.at[0, j])

    def load_up(j):
        return pltpu.make_async_copy(w_up.at[0, :, cols(j)], wgu.at[j, 0, pl.ds(HS, HS), :], load_sem.at[1, j])

    def load_down(j):
        return pltpu.make_async_copy(
            w_down.at[0, :, cols2(half, j)], wd.at[j, 0, pl.ds(0, HS), :], down_sem.at[j]
        )

    def store_out(j):
        return pltpu.make_async_copy(out_buf.at[j], out.at[0, :, cols2(0, j)], store_sem.at[j])

    def relay(j):
        return remote(blocks.at[0, :, cols(j)], arrived.at[j], relay_s.at[j], relay_r.at[j], next_section)

    def dispatch(d, j):
        step = (sign, -2 * sign, 3 * sign)[d - 1]
        part = pl.ds(d * CAP, CAP)
        return remote(
            picked.at[j, part, :], rows.at[j, part, :], disp_s.at[d - 1, j], disp_r.at[d - 1, j], at_y(step)
        )

    def keep(j):
        return pltpu.make_async_copy(
            picked.at[j, pl.ds(0, CAP), :], rows.at[j, pl.ds(0, CAP), :], load_sem.at[2, j]
        )

    def to_pair(j):
        return remote(
            rows.at[j, pl.ds(0, TOK), :], rows.at[j, pl.ds(TOK, TOK), :], pair_s.at[j], pair_r.at[j], pair
        )

    def ring(buf, count, sx, rx, sf, rf, sd, rd):
        mine = pl.ds(pl.multiple_of(core * count, count), count)

        def own(k, j):
            return remote(
                buf.at[j, 0, mine, :], buf.at[j, 2 - k, mine, :], sx.at[k, j], rx.at[k, j], at_x((1, -1)[k])
            )

        def forward(j):
            return remote(
                buf.at[j, 2 - core, mine, :], buf.at[j, 3, mine, :], sf.at[j], rf.at[j], at_x(1 - 2 * core)
            )

        def share(s, j):
            here = buf.at[j, s, mine, :]
            return remote(here, here, sd.at[s - 1, j], rd.at[s - 1, j], other_core)

        def share_in(s, j):
            theirs = buf.at[j, s, pl.ds(pl.multiple_of((1 - core) * count, count), count), :]
            return remote(theirs, theirs, sd.at[s - 1, j], rd.at[s - 1, j], other_core)

        return own, forward, share, share_in

    g_own, g_forward, g_share, g_share_in = ring(wgu, HS, gx_s, gx_r, gf_s, gf_r, gd_s, gd_r)
    d_own, d_forward, d_share, d_share_in = ring(wd, HS, dx_s, dx_r, df_s, df_r, dd_s, dd_r)

    def pair_down(j):
        return remote(
            w_down.at[0, :, cols2(1 - half, j)], wd.at[j, 0, pl.ds(HS, HS), :], pd_s.at[j], pd_r.at[j], pair
        )

    def core_down(j):
        part = wd.at[j, 0, pl.ds(HS, HS), :]
        return remote(part, part, pc_s.at[j], pc_r.at[j], other_core)

    def exchange(k):
        part = pl.ds((0, 4)[k], (4, 2)[k])
        return remote(packed_out.at[part], packed_in.at[part], act_s.at[k], act_r.at[k], pair)

    def home(src_row, d, slot, step, j):
        return remote(
            home_out.at[j, pl.ds(src_row, CAP), :], home_in.at[half * J2 + j, pl.ds(d * CAP, CAP), :],
            ret_s.at[slot, j], ret_r.at[d, half * J2 + j], at_y(step),
        )

    def homes(j):
        near = [home(d * CAP, d, d - 1, d * sign, j) for d in (1, 2, 3)]
        far = [home(TOK + d * CAP, d, 3 + d, -(1 + d) * sign, j) for d in range(4)]
        return near + far

    def home_arrival(d, g):
        part = home_in.at[g, pl.ds(d * CAP, CAP), :]
        return remote(part, part, ret_s.at[0, 0], ret_r.at[d, g], pair)

    def keep_home(j):
        return pltpu.make_async_copy(
            home_out.at[j, pl.ds(0, CAP), :], home_in.at[half * J2 + j, pl.ds(0, CAP), :], down_sem.at[J2 + j]
        )

    def each(fn, count=J):
        def body(j, carry):
            fn(j)
            return carry
        lax.fori_loop(0, count, body, 0)

    def staged(steps, stages, count=J):
        def body(t, carry):
            for lag, first, fn in stages:
                @pl.when((t >= lag + first) & (t < lag + count))
                def _(fn=fn, lag=lag):
                    fn(t - lag)
            return carry
        lax.fori_loop(0, steps, body, 0)

    def start_loads(j):
        load_gate(j).start()
        load_up(j).start()

    small = [
        pltpu.make_async_copy(src, dst, small_sem.at[k])
        for k, (src, dst) in enumerate(((ids_in.at[0], ids), (weights_in.at[0], weights), (gain_in, gain)))
    ]
    for copy in small:
        copy.start()
    each(start_loads)
    each(lambda j: load_down(j).start(), J2)

    barrier = pltpu.get_barrier_semaphore()
    partners = [next_section, last_section, other_core, at_x(1), at_x(-1)] + [at_y(k) for k in range(1, NY)]
    for partner in partners:
        pl.semaphore_signal(barrier, inc=1, device_id=partner, device_id_type=MESH)
    for copy in small:
        copy.wait()
    lane = lax.broadcasted_iota(jnp.int32, (TOK, TOK), 1)
    row = lax.broadcasted_iota(jnp.int32, (TOK, TOK), 0)
    group = row // CAP
    hop = jnp.where(group == 0, 0, jnp.where(group == 1, sign, jnp.where(group == 2, -2 * sign, 3 * sign)))
    slot_expert = ((y + hop + NY) % NY) // 2
    first = ids[0:1, :] == slot_expert
    second = ids[1:2, :] == slot_expert
    member = jnp.where(first | second, 1.0, 0.0)
    earlier = jnp.where(row < lane, 1.0, 0.0).astype(BF16)
    rank = jnp.dot(member.astype(BF16), earlier, preferred_element_type=F32)
    slot = (row % CAP).astype(F32)
    table = jnp.where(rank == slot, member, 0.0)
    gather_m[...] = table.astype(BF16)
    weighted = (table * jnp.where(first, weights[0:1, :], weights[1:2, :])).T
    high = weighted.astype(BF16)
    combine_hi[...] = high
    combine_lo[...] = (weighted - high.astype(F32)).astype(BF16)
    zero_pick = jnp.where(ids[...] >= EXPERTS, weights[...], 0.0)
    zero_sum = jnp.sum(zero_pick, axis=0, keepdims=True)
    zero_w[...] = jnp.broadcast_to(zero_sum, (TOK, TOK)).T

    acc[...] = jnp.zeros_like(acc)
    ssq[...] = jnp.zeros_like(ssq)
    home_ssq[...] = jnp.zeros_like(home_ssq)

    pl.semaphore_wait(barrier, len(partners))

    each(lambda j: relay(j).start())

    @pl.when(core == 1)
    def _():
        each(lambda j: pair_down(j).start(), J2)


    def send_first(j):
        load_gate(j).wait()
        load_up(j).wait()
        g_own(0, j).start()
        g_own(1, j).start()

    each(send_first)

    def squares(value):
        total = value[:, 0:128] * value[:, 0:128]
        for k in range(1, C // 128):
            piece = value[:, k * 128:(k + 1) * 128]
            total = total + piece * piece
        return total

    def pick_rows(j):
        relay(j).wait_recv()
        block = arrived[j]
        picked[j] = jnp.dot(gather_m[...], block, preferred_element_type=F32).astype(BF16)
        for d in (3, 2, 1):
            dispatch(d, j).start()
        keep(j).start()
        home_ssq[...] += squares(block.astype(F32))

    def pass_weights(j):
        g_own(0, j).wait_recv()
        g_own(1, j).wait_recv()
        g_forward(j).start()
        g_share(1, j).start()
        g_share(2, j).start()

    def pass_rows(j):
        keep(j).wait()
        for d in (1, 2, 3):
            dispatch(d, j).wait_recv()
        to_pair(j).start()

    def share_far(j):
        g_forward(j).wait_recv()
        g_share(3, j).start()

    def near_dots(j):
        to_pair(j).wait_recv()
        value = rows[j].astype(F32)
        ssq[...] += squares(value)
        scaled[j] = (value * gain[0:1, cols(j)].astype(F32)).astype(BF16)
        for s in (1, 2):
            g_share_in(s, j).wait_recv()
        acc[:, 0:NEAR] += lax.dot_general(
            scaled[j], wgu[j, 0:3].reshape(NEAR, C), (((1,), (1,)), ((), ())), preferred_element_type=F32
        )

    def far_dots(j):
        g_share_in(3, j).wait_recv()
        acc[:, NEAR:] += lax.dot_general(
            scaled[j], wgu[j, 3], (((1,), (1,)), ((), ())), preferred_element_type=F32
        )

    def ready_down(j):
        load_down(j).wait()

        @pl.when(core == 1)
        def _():
            pair_down(j).wait_recv()
            core_down(j).start()

    def send_down(j):
        d_own(0, j).start()
        d_own(1, j).start()

    def pass_down(j):
        d_own(0, j).wait_recv()
        d_own(1, j).wait_recv()
        d_forward(j).start()
        d_share(1, j).start()
        d_share(2, j).start()

    def share_down(j):
        d_forward(j).wait_recv()
        d_share(3, j).start()

    low = lax.broadcasted_iota(jnp.int32, (2 * TOK, 128), 1) < 64

    def activate(slots):
        inverse = lax.rsqrt(jnp.sum(ssq[...], axis=1, keepdims=True) * (1.0 / D) + 1e-06)
        for s in slots:
            base = s * 2 * HS
            gate = acc[:, base:base + 128] * inverse
            mid = acc[:, base + 128:base + 256] * inverse
            up = pltpu.roll(acc[:, base + 256:base + 384] * inverse, 64, 1)
            other = jnp.where(low, pltpu.roll(mid, 64, 1), up)
            main = (gate / (1.0 + jnp.exp(-gate)) * other).astype(BF16)
            tail = mid / (1.0 + jnp.exp(-mid)) * up
            hidden[s, :, 0:128] = main
            hidden[s, :, 128:192] = tail[:, 0:64].astype(BF16)
            packed_out[(0, 1, 2, 4)[s]] = main
            if s % 2 == 0:
                tail_two[...] = tail
            else:
                packed_out[s + 2] = jnp.where(low, tail_two[...], pltpu.roll(tail, 64, 1)).astype(BF16)

    def unpack():
        for to, start in ((0, TOK), (TOK, 0)):
            for s in range(NX):
                pair_hidden[s, to:to + TOK, 0:128] = packed_in[(0, 1, 2, 4)[s], start:start + TOK]
            for k in (3, 5):
                tails = packed_in[k, start:start + TOK].astype(F32)
                pair_hidden[k - 3, to:to + TOK, 128:192] = tails[:, 0:64].astype(BF16)
                pair_hidden[k - 2, to:to + TOK, 128:192] = pltpu.roll(tails, 64, 1)[:, 0:64].astype(BF16)

    def activate_near(j):
        activate(range(3))
        exchange(0).start()
        home_inv[...] = jnp.broadcast_to(
            lax.rsqrt(jnp.sum(home_ssq[...], axis=1, keepdims=True) * (1.0 / D) + 1e-06), (TOK, 128)
        )

    staged(J, [(0, 0, pick_rows), (1, 0, pass_rows), (0, 0, pass_weights), (2, 0, near_dots)])
    pass_rows(J - 1)
    each(ready_down, J2)
    send_down(0)
    send_down(1)
    staged(
        J,
        [(0, 0, share_far), (3 - J, J - 2, near_dots), (1, 0, far_dots), (4 - J, J - 1, activate_near)],
    )
    far_dots(J - 1)
    activate((3,))
    exchange(1).start()
    pass_down(0)
    send_down(2)
    pass_down(1)
    send_down(3)
    share_down(0)

    @pl.when(core == 0)
    def _():
        each(lambda j: core_down(j).wait_recv(), J2)

    exchange(0).wait_recv()
    exchange(1).wait_recv()
    unpack()

    def second_dots(j):
        for s in (1, 2, 3):
            d_share_in(s, j).wait_recv()
        total = jnp.dot(hidden[0], wd[j, 0, 0:HS, :], preferred_element_type=F32)
        total = total + jnp.dot(pair_hidden[0], wd[j, 0, HS:, :], preferred_element_type=F32)
        for s in range(1, NX):
            total = total + jnp.dot(hidden[s], wd[j, s, 0:HS, :], preferred_element_type=F32)
            total = total + jnp.dot(pair_hidden[s], wd[j, s, HS:, :], preferred_element_type=F32)
        home_out[j] = total.astype(BF16)
        for copy in homes(j)[::-1]:
            copy.start()
        keep_home(j).start()

    def finish(g):
        value = home_in[g]
        total = jnp.dot(combine_hi[...], value, preferred_element_type=F32)
        total = total + jnp.dot(combine_lo[...], value, preferred_element_type=F32)
        parts = C // C2
        lanes = pl.ds(pl.multiple_of(g % parts * C2, C2), C2)
        residual = arrived[g // parts, :, lanes].astype(F32)
        normed = (residual * home_inv[:, 0:1] * gain[0:1, cols2(0, g)].astype(F32)).astype(BF16)
        total = residual + zero_w[:, 0:1] * normed.astype(F32) + total
        out_buf[g] = total.astype(BF16)
        store_out(g).start()

    def finish_mine(j):
        g = half * J2 + j
        keep_home(j).wait()
        for d in (1, 2, 3):
            home_arrival(d, g).wait_recv()
        finish(g)

    def finish_other(j):
        g = (1 - half) * J2 + j
        for d in (0, 1, 2, 3):
            home_arrival(d, g).wait_recv()
        finish(g)

    staged(
        J2 + 2,
        [
            (0, 0, second_dots), (-2, 2, pass_down), (-4, 4, send_down), (-1, 1, share_down),
            (2, 0, finish_mine), (2, 0, finish_other),
        ],
        J2,
    )

    def drain(j):
        relay(j).wait_send()
        for d in (1, 2, 3):
            dispatch(d, j).wait_send()
        to_pair(j).wait_send()

    def drain_ring(own, forward, share, j):
        own(0, j).wait_send()
        own(1, j).wait_send()
        forward(j).wait_send()
        for s in (1, 2, 3):
            share(s, j).wait_send()

    def drain_home(j):
        for copy in homes(j):
            copy.wait_send()

    each(drain)
    each(lambda j: drain_ring(g_own, g_forward, g_share, j))
    each(lambda j: drain_ring(d_own, d_forward, d_share, j), J2)
    exchange(0).wait_send()
    exchange(1).wait_send()

    @pl.when(core == 1)
    def _():
        each(lambda j: pair_down(j).wait_send(), J2)
        each(lambda j: core_down(j).wait_send(), J2)

    each(drain_home, J2)
    each(lambda j: store_out(j).wait(), 2 * J2)


def local(blocks, norm_gain, w_gate, w_up, w_down, route_ids, route_weights):
    anywhere = pl.BlockSpec(memory_space=pl.ANY)
    dma = pltpu.SemaphoreType.DMA
    return pl.pallas_call(
        kernel,
        out_shape=jax.ShapeDtypeStruct(blocks.shape, blocks.dtype),
        in_specs=[anywhere] * 7,
        out_specs=anywhere,
        scratch_shapes=[
            pltpu.VMEM((1, D), BF16),
            pltpu.VMEM((2, TOK), jnp.int32),
            pltpu.VMEM((2, TOK), F32),
            pltpu.VMEM((J, TOK, C), BF16),
            pltpu.VMEM((J, TOK, C), BF16),
            pltpu.VMEM((J, 2 * TOK, C), BF16),
            pltpu.VMEM((J, NX, 2 * HS, C), BF16),
            pltpu.VMEM((J2, NX, 2 * HS, C2), BF16),
            pltpu.VMEM((J, 2 * TOK, C), BF16),
            pltpu.VMEM((2 * TOK, NX * 2 * HS), F32),
            pltpu.VMEM((2 * TOK, 128), F32),
            pltpu.VMEM((TOK, 128), F32),
            pltpu.VMEM((NX, 2 * TOK, HS), BF16),
            pltpu.VMEM((NX, 2 * TOK, HS), BF16),
            pltpu.VMEM((6, 2 * TOK, 128), BF16),
            pltpu.VMEM((6, 2 * TOK, 128), BF16),
            pltpu.VMEM((2 * TOK, 128), F32),
            pltpu.VMEM((J2, 2 * TOK, C2), BF16),
            pltpu.VMEM((2 * J2, TOK, C2), BF16),
            pltpu.VMEM((2 * J2, TOK, C2), BF16),
            pltpu.VMEM((TOK, TOK), BF16),
            pltpu.VMEM((TOK, TOK), BF16),
            pltpu.VMEM((TOK, TOK), BF16),
            pltpu.VMEM((TOK, 128), F32),
            pltpu.VMEM((TOK, 128), F32),
            dma((3,)), dma((3, J)), dma((2 * J2,)), dma((2 * J2,)),
            dma((J,)), dma((J,)), dma((3, J)), dma((3, J)), dma((J,)), dma((J,)),
            dma((2, J)), dma((2, J)), dma((J,)), dma((J,)), dma((3, J)), dma((3, J)),
            dma((2, J2)), dma((2, J2)), dma((J2,)), dma((J2,)), dma((3, J2)), dma((3, J2)),
            dma((J2,)), dma((J2,)), dma((J2,)), dma((J2,)), dma((2,)), dma((2,)),
            dma((7, J2)), dma((4, 2 * J2)),
        ],
        compiler_params=pltpu.CompilerParams(
            collective_id=0, has_side_effects=True, vmem_limit_bytes=60 * 1024 * 1024
        ),
        cost_estimate=pl.CostEstimate(
            flops=2 * 3 * 1024 * D * HS, bytes_accessed=6 * 1024 * 1024, transcendentals=256 * 768
        ),
    )(
        blocks, norm_gain, jnp.swapaxes(w_gate, 1, 2), jnp.swapaxes(w_up, 1, 2), w_down,
        jnp.swapaxes(route_ids, 1, 2), jnp.swapaxes(route_weights, 1, 2),
    )


def solution(mesh):
    placed = (
        P("section", ("dp", "expert"), None),
        P("section", None),
        P("section", None, "expert"),
        P("section", None, "expert"),
        P("section", "expert", None),
        P("section", ("dp", "expert"), None),
        P("section", ("dp", "expert"), None),
    )
    return jax.shard_map(
        local,
        mesh=mesh,
        in_specs=placed,
        out_specs=P("section", ("dp", "expert"), None),
        check_vma=False,
    )
```

```python
import jax
import jax.numpy as jnp
from jax import lax
from jax.experimental import pallas as pl
from jax.experimental.pallas import tpu as pltpu
from jax.sharding import PartitionSpec as P

D = 3072
HS = 192
EXPERTS = 4
CAP = 32
TOK = 128
NX = 4
NY = 8
C = 512
J = D // C
C2 = 256
WIDE = D // 2
J2 = WIDE // C2
NEAR = 3 * 2 * HS
MESH = pl.DeviceIdType.MESH
F32 = jnp.float32
BF16 = jnp.bfloat16


def kernel(
    blocks, gain_in, w_gate, w_up, w_down, ids_in, weights_in, out,
    gain, ids, weights, arrived, picked, rows, wgu, wd, scaled, acc, ssq, home_ssq,
    hidden, pair_hidden, packed_out, packed_in, tail_two, home_out, home_in, out_buf,
    gather_m, combine_hi, combine_lo, zero_w, home_inv,
    small_sem, load_sem, down_sem, store_sem, relay_s, relay_r, disp_s, disp_r, pair_s, pair_r,
    gx_s, gx_r, gf_s, gf_r, gd_s, gd_r, dx_s, dx_r, df_s, df_r, dd_s, dd_r,
    pd_s, pd_r, pc_s, pc_r, act_s, act_r, ret_s, ret_r,
):
    section = lax.axis_index("section")
    sections = lax.axis_size("section")
    place = lax.axis_index("expert")
    core = lax.axis_index("dp")
    y = place // NX
    x = place % NX
    sign = 2 * (y % 2) - 1

    def at_x(step):
        return {"expert": y * NX + (x + step + NX) % NX}

    def at_y(step):
        return {"expert": ((y + step + NY) % NY) * NX + x}

    next_section = {"section": (section + 1) % sections}
    last_section = {"section": (section + sections - 1) % sections}
    other_core = {"dp": 1 - core}
    pair = at_y(-sign)
    half = y % 2

    def remote(src, dst, send, recv, target):
        return pltpu.make_async_remote_copy(
            src_ref=src, dst_ref=dst, send_sem=send, recv_sem=recv,
            device_id=target, device_id_type=MESH,
        )

    def cols(j):
        return pl.ds(pl.multiple_of(j * C, C), C)

    def cols2(side, j):
        return pl.ds(pl.multiple_of(side * WIDE + j * C2, C2), C2)

    def load_gate(j):
        return pltpu.make_async_copy(w_gate.at[0, :, cols(j)], wgu.at[j, 0, pl.ds(0, HS), :], load_sem.at[0, j])

    def load_up(j):
        return pltpu.make_async_copy(w_up.at[0, :, cols(j)], wgu.at[j, 0, pl.ds(HS, HS), :], load_sem.at[1, j])

    def load_down(j):
        return pltpu.make_async_copy(
            w_down.at[0, :, cols2(half, j)], wd.at[j, 0, pl.ds(0, HS), :], down_sem.at[j]
        )

    def store_out(j):
        return pltpu.make_async_copy(out_buf.at[j], out.at[0, :, cols2(0, j)], store_sem.at[j])

    def relay(j):
        return remote(blocks.at[0, :, cols(j)], arrived.at[j], relay_s.at[j], relay_r.at[j], next_section)

    def dispatch(d, j):
        step = (sign, -2 * sign, 3 * sign)[d - 1]
        part = pl.ds(d * CAP, CAP)
        return remote(
            picked.at[j, part, :], rows.at[j, part, :], disp_s.at[d - 1, j], disp_r.at[d - 1, j], at_y(step)
        )

    def keep(j):
        return pltpu.make_async_copy(
            picked.at[j, pl.ds(0, CAP), :], rows.at[j, pl.ds(0, CAP), :], load_sem.at[2, j]
        )

    def to_pair(j):
        return remote(
            rows.at[j, pl.ds(0, TOK), :], rows.at[j, pl.ds(TOK, TOK), :], pair_s.at[j], pair_r.at[j], pair
        )

    def ring(buf, count, sx, rx, sf, rf, sd, rd):
        mine = pl.ds(pl.multiple_of(core * count, count), count)

        def own(k, j):
            return remote(
                buf.at[j, 0, mine, :], buf.at[j, 2 - k, mine, :], sx.at[k, j], rx.at[k, j], at_x((1, -1)[k])
            )

        def forward(j):
            return remote(
                buf.at[j, 2 - core, mine, :], buf.at[j, 3, mine, :], sf.at[j], rf.at[j], at_x(1 - 2 * core)
            )

        def share(s, j):
            here = buf.at[j, s, mine, :]
            return remote(here, here, sd.at[s - 1, j], rd.at[s - 1, j], other_core)

        def share_in(s, j):
            theirs = buf.at[j, s, pl.ds(pl.multiple_of((1 - core) * count, count), count), :]
            return remote(theirs, theirs, sd.at[s - 1, j], rd.at[s - 1, j], other_core)

        return own, forward, share, share_in

    g_own, g_forward, g_share, g_share_in = ring(wgu, HS, gx_s, gx_r, gf_s, gf_r, gd_s, gd_r)
    d_own, d_forward, d_share, d_share_in = ring(wd, HS, dx_s, dx_r, df_s, df_r, dd_s, dd_r)

    def pair_down(j):
        return remote(
            w_down.at[0, :, cols2(1 - half, j)], wd.at[j, 0, pl.ds(HS, HS), :], pd_s.at[j], pd_r.at[j], pair
        )

    def core_down(j):
        part = wd.at[j, 0, pl.ds(HS, HS), :]
        return remote(part, part, pc_s.at[j], pc_r.at[j], other_core)

    def exchange(k):
        part = pl.ds((0, 4)[k], (4, 2)[k])
        return remote(packed_out.at[part], packed_in.at[part], act_s.at[k], act_r.at[k], pair)

    def home(src_row, d, slot, step, j):
        return remote(
            home_out.at[j, pl.ds(src_row, CAP), :], home_in.at[half * J2 + j, pl.ds(d * CAP, CAP), :],
            ret_s.at[slot, j], ret_r.at[d, half * J2 + j], at_y(step),
        )

    def homes(j):
        near = [home(d * CAP, d, d - 1, d * sign, j) for d in (1, 2, 3)]
        far = [home(TOK + d * CAP, d, 3 + d, -(1 + d) * sign, j) for d in range(4)]
        return near + far

    def home_arrival(d, g):
        part = home_in.at[g, pl.ds(d * CAP, CAP), :]
        return remote(part, part, ret_s.at[0, 0], ret_r.at[d, g], pair)

    def keep_home(j):
        return pltpu.make_async_copy(
            home_out.at[j, pl.ds(0, CAP), :], home_in.at[half * J2 + j, pl.ds(0, CAP), :], down_sem.at[J2 + j]
        )

    def each(fn, count=J):
        def body(j, carry):
            fn(j)
            return carry
        lax.fori_loop(0, count, body, 0)

    def staged(steps, stages, count=J):
        def body(t, carry):
            for lag, first, fn in stages:
                @pl.when((t >= lag + first) & (t < lag + count))
                def _(fn=fn, lag=lag):
                    fn(t - lag)
            return carry
        lax.fori_loop(0, steps, body, 0)

    def start_loads(j):
        load_gate(j).start()
        load_up(j).start()

    small = [
        pltpu.make_async_copy(src, dst, small_sem.at[k])
        for k, (src, dst) in enumerate(((ids_in.at[0], ids), (weights_in.at[0], weights), (gain_in, gain)))
    ]
    for copy in small:
        copy.start()
    each(start_loads)
    each(lambda j: load_down(j).start(), J2)

    barrier = pltpu.get_barrier_semaphore()
    partners = [next_section, last_section, other_core, at_x(1), at_x(-1)] + [at_y(k) for k in range(1, NY)]
    for partner in partners:
        pl.semaphore_signal(barrier, inc=1, device_id=partner, device_id_type=MESH)
    for copy in small:
        copy.wait()
    lane = lax.broadcasted_iota(jnp.int32, (TOK, TOK), 1)
    row = lax.broadcasted_iota(jnp.int32, (TOK, TOK), 0)
    group = row // CAP
    hop = jnp.where(group == 0, 0, jnp.where(group == 1, sign, jnp.where(group == 2, -2 * sign, 3 * sign)))
    slot_expert = ((y + hop + NY) % NY) // 2
    first = ids[0:1, :] == slot_expert
    second = ids[1:2, :] == slot_expert
    member = jnp.where(first | second, 1.0, 0.0)
    earlier = jnp.where(row < lane, 1.0, 0.0).astype(BF16)
    rank = jnp.dot(member.astype(BF16), earlier, preferred_element_type=F32)
    slot = (row % CAP).astype(F32)
    table = jnp.where(rank == slot, member, 0.0)
    gather_m[...] = table.astype(BF16)
    weighted = (table * jnp.where(first, weights[0:1, :], weights[1:2, :])).T
    high = weighted.astype(BF16)
    combine_hi[...] = high
    combine_lo[...] = (weighted - high.astype(F32)).astype(BF16)
    zero_pick = jnp.where(ids[...] >= EXPERTS, weights[...], 0.0)
    zero_sum = jnp.sum(zero_pick, axis=0, keepdims=True)
    zero_w[...] = jnp.broadcast_to(zero_sum, (TOK, TOK)).T

    acc[...] = jnp.zeros_like(acc)
    ssq[...] = jnp.zeros_like(ssq)
    home_ssq[...] = jnp.zeros_like(home_ssq)

    pl.semaphore_wait(barrier, len(partners))

    each(lambda j: relay(j).start())

    @pl.when(core == 1)
    def _():
        each(lambda j: pair_down(j).start(), J2)


    def send_first(j):
        load_gate(j).wait()
        load_up(j).wait()
        g_own(0, j).start()
        g_own(1, j).start()

    each(send_first)

    def squares(value):
        total = value[:, 0:128] * value[:, 0:128]
        for k in range(1, C // 128):
            piece = value[:, k * 128:(k + 1) * 128]
            total = total + piece * piece
        return total

    def pick_rows(j):
        relay(j).wait_recv()
        block = arrived[j]
        picked[j] = jnp.dot(gather_m[...], block, preferred_element_type=F32).astype(BF16)
        for d in (3, 2, 1):
            dispatch(d, j).start()
        keep(j).start()
        home_ssq[...] += squares(block.astype(F32))

    def pass_weights(j):
        g_own(0, j).wait_recv()
        g_own(1, j).wait_recv()
        g_forward(j).start()
        g_share(1, j).start()
        g_share(2, j).start()

    def pass_rows(j):
        keep(j).wait()
        for d in (1, 2, 3):
            dispatch(d, j).wait_recv()
        to_pair(j).start()

    def share_far(j):
        g_forward(j).wait_recv()
        g_share(3, j).start()

    def near_dots(j):
        to_pair(j).wait_recv()
        value = rows[j].astype(F32)
        ssq[...] += squares(value)
        scaled[j] = (value * gain[0:1, cols(j)].astype(F32)).astype(BF16)
        for s in (1, 2):
            g_share_in(s, j).wait_recv()
        acc[:, 0:NEAR] += lax.dot_general(
            scaled[j], wgu[j, 0:3].reshape(NEAR, C), (((1,), (1,)), ((), ())), preferred_element_type=F32
        )

    def far_dots(j):
        g_share_in(3, j).wait_recv()
        acc[:, NEAR:] += lax.dot_general(
            scaled[j], wgu[j, 3], (((1,), (1,)), ((), ())), preferred_element_type=F32
        )

    def ready_down(j):
        load_down(j).wait()

        @pl.when(core == 1)
        def _():
            pair_down(j).wait_recv()
            core_down(j).start()

    def send_down(j):
        d_own(0, j).start()
        d_own(1, j).start()

    def pass_down(j):
        d_own(0, j).wait_recv()
        d_own(1, j).wait_recv()
        d_forward(j).start()
        d_share(1, j).start()
        d_share(2, j).start()

    def share_down(j):
        d_forward(j).wait_recv()
        d_share(3, j).start()

    low = lax.broadcasted_iota(jnp.int32, (2 * TOK, 128), 1) < 64

    def activate(slots):
        inverse = lax.rsqrt(jnp.sum(ssq[...], axis=1, keepdims=True) * (1.0 / D) + 1e-06)
        for s in slots:
            base = s * 2 * HS
            gate = acc[:, base:base + 128] * inverse
            mid = acc[:, base + 128:base + 256] * inverse
            up = pltpu.roll(acc[:, base + 256:base + 384] * inverse, 64, 1)
            other = jnp.where(low, pltpu.roll(mid, 64, 1), up)
            main = (gate / (1.0 + jnp.exp(-gate)) * other).astype(BF16)
            tail = mid / (1.0 + jnp.exp(-mid)) * up
            hidden[s, :, 0:128] = main
            hidden[s, :, 128:192] = tail[:, 0:64].astype(BF16)
            packed_out[(0, 1, 2, 4)[s]] = main
            if s % 2 == 0:
                tail_two[...] = tail
            else:
                packed_out[s + 2] = jnp.where(low, tail_two[...], pltpu.roll(tail, 64, 1)).astype(BF16)

    def unpack():
        for to, start in ((0, TOK), (TOK, 0)):
            for s in range(NX):
                pair_hidden[s, to:to + TOK, 0:128] = packed_in[(0, 1, 2, 4)[s], start:start + TOK]
            for k in (3, 5):
                tails = packed_in[k, start:start + TOK].astype(F32)
                pair_hidden[k - 3, to:to + TOK, 128:192] = tails[:, 0:64].astype(BF16)
                pair_hidden[k - 2, to:to + TOK, 128:192] = pltpu.roll(tails, 64, 1)[:, 0:64].astype(BF16)

    def activate_near(j):
        activate(range(3))
        exchange(0).start()
        home_inv[...] = jnp.broadcast_to(
            lax.rsqrt(jnp.sum(home_ssq[...], axis=1, keepdims=True) * (1.0 / D) + 1e-06), (TOK, 128)
        )

    staged(J, [(0, 0, pick_rows), (1, 0, pass_rows), (0, 0, pass_weights), (2, 0, near_dots)])
    pass_rows(J - 1)
    each(ready_down, J2)
    send_down(0)
    send_down(1)
    staged(
        J,
        [(0, 0, share_far), (3 - J, J - 2, near_dots), (1, 0, far_dots), (4 - J, J - 1, activate_near)],
    )
    pass_down(0)
    send_down(2)
    far_dots(J - 1)
    activate((3,))
    exchange(1).start()
    pass_down(1)
    send_down(3)
    share_down(0)

    @pl.when(core == 0)
    def _():
        each(lambda j: core_down(j).wait_recv(), J2)

    def drain(j):
        relay(j).wait_send()
        for d in (1, 2, 3):
            dispatch(d, j).wait_send()
        to_pair(j).wait_send()

    def drain_ring(own, forward, share, j):
        own(0, j).wait_send()
        own(1, j).wait_send()
        forward(j).wait_send()
        for s in (1, 2, 3):
            share(s, j).wait_send()

    def drain_home(j):
        for copy in homes(j):
            copy.wait_send()

    def drain_second(j):
        drain_ring(d_own, d_forward, d_share, j)
        drain_home(j)

    each(drain)
    each(lambda j: drain_ring(g_own, g_forward, g_share, j))

    @pl.when(core == 1)
    def _():
        each(lambda j: pair_down(j).wait_send(), J2)
        each(lambda j: core_down(j).wait_send(), J2)

    exchange(0).wait_recv()
    exchange(1).wait_recv()
    unpack()
    exchange(0).wait_send()
    exchange(1).wait_send()

    def second_dots(j):
        for s in (1, 2, 3):
            d_share_in(s, j).wait_recv()
        total = jnp.dot(hidden[0], wd[j, 0, 0:HS, :], preferred_element_type=F32)
        total = total + jnp.dot(pair_hidden[0], wd[j, 0, HS:, :], preferred_element_type=F32)
        for s in range(1, NX):
            total = total + jnp.dot(hidden[s], wd[j, s, 0:HS, :], preferred_element_type=F32)
            total = total + jnp.dot(pair_hidden[s], wd[j, s, HS:, :], preferred_element_type=F32)
        home_out[j] = total.astype(BF16)
        for copy in homes(j)[::-1]:
            copy.start()
        keep_home(j).start()

    def finish(g):
        value = home_in[g]
        total = jnp.dot(combine_hi[...], value, preferred_element_type=F32)
        total = total + jnp.dot(combine_lo[...], value, preferred_element_type=F32)
        parts = C // C2
        lanes = pl.ds(pl.multiple_of(g % parts * C2, C2), C2)
        residual = arrived[g // parts, :, lanes].astype(F32)
        normed = (residual * home_inv[:, 0:1] * gain[0:1, cols2(0, g)].astype(F32)).astype(BF16)
        total = residual + zero_w[:, 0:1] * normed.astype(F32) + total
        out_buf[g] = total.astype(BF16)
        store_out(g).start()

    def finish_mine(j):
        g = half * J2 + j
        keep_home(j).wait()
        for d in (1, 2, 3):
            home_arrival(d, g).wait_recv()
        finish(g)

    def finish_other(j):
        g = (1 - half) * J2 + j
        for d in (0, 1, 2, 3):
            home_arrival(d, g).wait_recv()
        finish(g)

    staged(
        J2 + 2,
        [
            (0, 0, second_dots), (-2, 2, pass_down), (-4, 4, send_down), (-1, 1, share_down),
            (2, 0, drain_second), (2, 0, finish_mine), (2, 0, finish_other),
        ],
        J2,
    )

    each(lambda j: store_out(j).wait(), 2 * J2)


def local(blocks, norm_gain, w_gate, w_up, w_down, route_ids, route_weights):
    anywhere = pl.BlockSpec(memory_space=pl.ANY)
    dma = pltpu.SemaphoreType.DMA
    return pl.pallas_call(
        kernel,
        out_shape=jax.ShapeDtypeStruct(blocks.shape, blocks.dtype),
        in_specs=[anywhere] * 7,
        out_specs=anywhere,
        scratch_shapes=[
            pltpu.VMEM((1, D), BF16),
            pltpu.VMEM((2, TOK), jnp.int32),
            pltpu.VMEM((2, TOK), F32),
            pltpu.VMEM((J, TOK, C), BF16),
            pltpu.VMEM((J, TOK, C), BF16),
            pltpu.VMEM((J, 2 * TOK, C), BF16),
            pltpu.VMEM((J, NX, 2 * HS, C), BF16),
            pltpu.VMEM((J2, NX, 2 * HS, C2), BF16),
            pltpu.VMEM((J, 2 * TOK, C), BF16),
            pltpu.VMEM((2 * TOK, NX * 2 * HS), F32),
            pltpu.VMEM((2 * TOK, 128), F32),
            pltpu.VMEM((TOK, 128), F32),
            pltpu.VMEM((NX, 2 * TOK, HS), BF16),
            pltpu.VMEM((NX, 2 * TOK, HS), BF16),
            pltpu.VMEM((6, 2 * TOK, 128), BF16),
            pltpu.VMEM((6, 2 * TOK, 128), BF16),
            pltpu.VMEM((2 * TOK, 128), F32),
            pltpu.VMEM((J2, 2 * TOK, C2), BF16),
            pltpu.VMEM((2 * J2, TOK, C2), BF16),
            pltpu.VMEM((2 * J2, TOK, C2), BF16),
            pltpu.VMEM((TOK, TOK), BF16),
            pltpu.VMEM((TOK, TOK), BF16),
            pltpu.VMEM((TOK, TOK), BF16),
            pltpu.VMEM((TOK, 128), F32),
            pltpu.VMEM((TOK, 128), F32),
            dma((3,)), dma((3, J)), dma((2 * J2,)), dma((2 * J2,)),
            dma((J,)), dma((J,)), dma((3, J)), dma((3, J)), dma((J,)), dma((J,)),
            dma((2, J)), dma((2, J)), dma((J,)), dma((J,)), dma((3, J)), dma((3, J)),
            dma((2, J2)), dma((2, J2)), dma((J2,)), dma((J2,)), dma((3, J2)), dma((3, J2)),
            dma((J2,)), dma((J2,)), dma((J2,)), dma((J2,)), dma((2,)), dma((2,)),
            dma((7, J2)), dma((4, 2 * J2)),
        ],
        compiler_params=pltpu.CompilerParams(
            collective_id=0, has_side_effects=True, vmem_limit_bytes=60 * 1024 * 1024
        ),
        cost_estimate=pl.CostEstimate(
            flops=2 * 3 * 1024 * D * HS, bytes_accessed=6 * 1024 * 1024, transcendentals=256 * 768
        ),
    )(
        blocks, norm_gain, jnp.swapaxes(w_gate, 1, 2), jnp.swapaxes(w_up, 1, 2), w_down,
        jnp.swapaxes(route_ids, 1, 2), jnp.swapaxes(route_weights, 1, 2),
    )


def solution(mesh):
    placed = (
        P("section", ("dp", "expert"), None),
        P("section", None),
        P("section", None, "expert"),
        P("section", None, "expert"),
        P("section", "expert", None),
        P("section", ("dp", "expert"), None),
        P("section", ("dp", "expert"), None),
    )
    return jax.shard_map(
        local,
        mesh=mesh,
        in_specs=placed,
        out_specs=P("section", ("dp", "expert"), None),
        check_vma=False,
    )
```

```python
import jax
import jax.numpy as jnp
from jax import lax
from jax.experimental import pallas as pl
from jax.experimental.pallas import tpu as pltpu
from jax.sharding import PartitionSpec as P

D = 3072
HS = 192
EXPERTS = 4
CAP = 32
TOK = 128
NX = 4
NY = 8
C = 512
J = D // C
C2 = 256
WIDE = D // 2
J2 = WIDE // C2
NEAR = 3 * 2 * HS
MESH = pl.DeviceIdType.MESH
F32 = jnp.float32
BF16 = jnp.bfloat16


def kernel(
    blocks, gain_in, w_gate, w_up, w_down, ids_in, weights_in, out,
    gain, ids, weights, arrived, picked, rows, wgu, wd, scaled, acc, ssq, home_ssq,
    hidden, pair_hidden, packed_out, packed_in, tail_two, home_out, home_in, start, out_buf,
    gather_m, combine_hi, combine_lo, zero_w, home_inv,
    small_sem, load_sem, down_sem, store_sem, relay_s, relay_r, disp_s, disp_r, pair_s, pair_r,
    gx_s, gx_r, gf_s, gf_r, gd_s, gd_r, dx_s, dx_r, df_s, df_r, dd_s, dd_r,
    pd_s, pd_r, pc_s, pc_r, act_s, act_r, ret_s, ret_r,
):
    section = lax.axis_index("section")
    sections = lax.axis_size("section")
    place = lax.axis_index("expert")
    core = lax.axis_index("dp")
    y = place // NX
    x = place % NX
    sign = 2 * (y % 2) - 1

    def at_x(step):
        return {"expert": y * NX + (x + step + NX) % NX}

    def at_y(step):
        return {"expert": ((y + step + NY) % NY) * NX + x}

    next_section = {"section": (section + 1) % sections}
    last_section = {"section": (section + sections - 1) % sections}
    other_core = {"dp": 1 - core}
    pair = at_y(-sign)
    half = y % 2

    def remote(src, dst, send, recv, target):
        return pltpu.make_async_remote_copy(
            src_ref=src, dst_ref=dst, send_sem=send, recv_sem=recv,
            device_id=target, device_id_type=MESH,
        )

    def cols(j):
        return pl.ds(pl.multiple_of(j * C, C), C)

    def cols2(side, j):
        return pl.ds(pl.multiple_of(side * WIDE + j * C2, C2), C2)

    def load_gate(j):
        return pltpu.make_async_copy(w_gate.at[0, :, cols(j)], wgu.at[j, 0, pl.ds(0, HS), :], load_sem.at[0, j])

    def load_up(j):
        return pltpu.make_async_copy(w_up.at[0, :, cols(j)], wgu.at[j, 0, pl.ds(HS, HS), :], load_sem.at[1, j])

    def load_down(j):
        return pltpu.make_async_copy(
            w_down.at[0, :, cols2(half, j)], wd.at[j, 0, pl.ds(0, HS), :], down_sem.at[j]
        )

    def store_out(j):
        return pltpu.make_async_copy(out_buf.at[j], out.at[0, :, cols2(0, j)], store_sem.at[j])

    def relay(j):
        return remote(blocks.at[0, :, cols(j)], arrived.at[j], relay_s.at[j], relay_r.at[j], next_section)

    def dispatch(d, j):
        step = (sign, -2 * sign, 3 * sign)[d - 1]
        part = pl.ds(d * CAP, CAP)
        return remote(
            picked.at[j, part, :], rows.at[j, part, :], disp_s.at[d - 1, j], disp_r.at[d - 1, j], at_y(step)
        )

    def keep(j):
        return pltpu.make_async_copy(
            picked.at[j, pl.ds(0, CAP), :], rows.at[j, pl.ds(0, CAP), :], load_sem.at[2, j]
        )

    def to_pair(j):
        return remote(
            rows.at[j, pl.ds(0, TOK), :], rows.at[j, pl.ds(TOK, TOK), :], pair_s.at[j], pair_r.at[j], pair
        )

    def ring(buf, count, sx, rx, sf, rf, sd, rd):
        mine = pl.ds(pl.multiple_of(core * count, count), count)

        def own(k, j):
            return remote(
                buf.at[j, 0, mine, :], buf.at[j, 2 - k, mine, :], sx.at[k, j], rx.at[k, j], at_x((1, -1)[k])
            )

        def forward(j):
            return remote(
                buf.at[j, 2 - core, mine, :], buf.at[j, 3, mine, :], sf.at[j], rf.at[j], at_x(1 - 2 * core)
            )

        def share(s, j):
            here = buf.at[j, s, mine, :]
            return remote(here, here, sd.at[s - 1, j], rd.at[s - 1, j], other_core)

        def share_in(s, j):
            theirs = buf.at[j, s, pl.ds(pl.multiple_of((1 - core) * count, count), count), :]
            return remote(theirs, theirs, sd.at[s - 1, j], rd.at[s - 1, j], other_core)

        return own, forward, share, share_in

    g_own, g_forward, g_share, g_share_in = ring(wgu, HS, gx_s, gx_r, gf_s, gf_r, gd_s, gd_r)
    d_own, d_forward, d_share, d_share_in = ring(wd, HS, dx_s, dx_r, df_s, df_r, dd_s, dd_r)

    def pair_down(j):
        return remote(
            w_down.at[0, :, cols2(1 - half, j)], wd.at[j, 0, pl.ds(HS, HS), :], pd_s.at[j], pd_r.at[j], pair
        )

    def core_down(j):
        part = wd.at[j, 0, pl.ds(HS, HS), :]
        return remote(part, part, pc_s.at[j], pc_r.at[j], other_core)

    def exchange(k):
        part = pl.ds((0, 4)[k], (4, 2)[k])
        return remote(packed_out.at[part], packed_in.at[part], act_s.at[k], act_r.at[k], pair)

    def home(src_row, d, slot, step, j):
        return remote(
            home_out.at[j, pl.ds(src_row, CAP), :], home_in.at[half * J2 + j, pl.ds(d * CAP, CAP), :],
            ret_s.at[slot, j], ret_r.at[d, half * J2 + j], at_y(step),
        )

    def homes(j):
        near = [home(d * CAP, d, d - 1, d * sign, j) for d in (1, 2, 3)]
        far = [home(TOK + d * CAP, d, 3 + d, -(1 + d) * sign, j) for d in range(4)]
        return near + far

    def home_arrival(d, g):
        part = home_in.at[g, pl.ds(d * CAP, CAP), :]
        return remote(part, part, ret_s.at[0, 0], ret_r.at[d, g], pair)

    def keep_home(j):
        return pltpu.make_async_copy(
            home_out.at[j, pl.ds(0, CAP), :], home_in.at[half * J2 + j, pl.ds(0, CAP), :], down_sem.at[J2 + j]
        )

    def each(fn, count=J):
        def body(j, carry):
            fn(j)
            return carry
        lax.fori_loop(0, count, body, 0)

    def staged(steps, stages, count=J):
        def body(t, carry):
            for lag, first, fn in stages:
                @pl.when((t >= lag + first) & (t < lag + count))
                def _(fn=fn, lag=lag):
                    fn(t - lag)
            return carry
        lax.fori_loop(0, steps, body, 0)

    def start_loads(j):
        load_gate(j).start()
        load_up(j).start()

    small = [
        pltpu.make_async_copy(src, dst, small_sem.at[k])
        for k, (src, dst) in enumerate(((ids_in.at[0], ids), (weights_in.at[0], weights), (gain_in, gain)))
    ]
    for copy in small:
        copy.start()
    each(start_loads)
    each(lambda j: load_down(j).start(), J2)

    barrier = pltpu.get_barrier_semaphore()
    partners = [next_section, last_section, other_core, at_x(1), at_x(-1)] + [at_y(k) for k in range(1, NY)]
    for partner in partners:
        pl.semaphore_signal(barrier, inc=1, device_id=partner, device_id_type=MESH)
    for copy in small:
        copy.wait()
    lane = lax.broadcasted_iota(jnp.int32, (TOK, TOK), 1)
    row = lax.broadcasted_iota(jnp.int32, (TOK, TOK), 0)
    group = row // CAP
    hop = jnp.where(group == 0, 0, jnp.where(group == 1, sign, jnp.where(group == 2, -2 * sign, 3 * sign)))
    slot_expert = ((y + hop + NY) % NY) // 2
    first = ids[0:1, :] == slot_expert
    second = ids[1:2, :] == slot_expert
    member = jnp.where(first | second, 1.0, 0.0)
    earlier = jnp.where(row < lane, 1.0, 0.0).astype(BF16)
    rank = jnp.dot(member.astype(BF16), earlier, preferred_element_type=F32)
    slot = (row % CAP).astype(F32)
    table = jnp.where(rank == slot, member, 0.0)
    gather_m[...] = table.astype(BF16)
    weighted = (table * jnp.where(first, weights[0:1, :], weights[1:2, :])).T
    high = weighted.astype(BF16)
    combine_hi[...] = high
    combine_lo[...] = (weighted - high.astype(F32)).astype(BF16)
    zero_pick = jnp.where(ids[...] >= EXPERTS, weights[...], 0.0)
    zero_sum = jnp.sum(zero_pick, axis=0, keepdims=True)
    zero_w[...] = jnp.broadcast_to(zero_sum, (TOK, TOK)).T

    acc[...] = jnp.zeros_like(acc)
    ssq[...] = jnp.zeros_like(ssq)
    home_ssq[...] = jnp.zeros_like(home_ssq)

    pl.semaphore_wait(barrier, len(partners))

    each(lambda j: relay(j).start())

    @pl.when(core == 1)
    def _():
        each(lambda j: pair_down(j).start(), J2)


    def send_first(j):
        load_gate(j).wait()
        load_up(j).wait()
        g_own(0, j).start()
        g_own(1, j).start()

    each(send_first)

    def squares(value):
        total = value[:, 0:128] * value[:, 0:128]
        for k in range(1, C // 128):
            piece = value[:, k * 128:(k + 1) * 128]
            total = total + piece * piece
        return total

    def pick_rows(j):
        relay(j).wait_recv()
        block = arrived[j]
        picked[j] = jnp.dot(gather_m[...], block, preferred_element_type=F32).astype(BF16)
        for d in (3, 2, 1):
            dispatch(d, j).start()
        keep(j).start()
        home_ssq[...] += squares(block.astype(F32))

    def pass_weights(j):
        g_own(0, j).wait_recv()
        g_own(1, j).wait_recv()
        g_forward(j).start()
        g_share(1, j).start()
        g_share(2, j).start()

    def pass_rows(j):
        keep(j).wait()
        for d in (1, 2, 3):
            dispatch(d, j).wait_recv()
        to_pair(j).start()

    def share_far(j):
        g_forward(j).wait_recv()
        g_share(3, j).start()

    def near_dots(j):
        to_pair(j).wait_recv()
        value = rows[j].astype(F32)
        ssq[...] += squares(value)
        scaled[j] = (value * gain[0:1, cols(j)].astype(F32)).astype(BF16)
        for s in (1, 2):
            g_share_in(s, j).wait_recv()
        acc[:, 0:NEAR] += lax.dot_general(
            scaled[j], wgu[j, 0:3].reshape(NEAR, C), (((1,), (1,)), ((), ())), preferred_element_type=F32
        )

    def far_dots(j):
        g_share_in(3, j).wait_recv()
        acc[:, NEAR:] += lax.dot_general(
            scaled[j], wgu[j, 3], (((1,), (1,)), ((), ())), preferred_element_type=F32
        )

    def ready_down(j):
        load_down(j).wait()

        @pl.when(core == 1)
        def _():
            pair_down(j).wait_recv()
            core_down(j).start()

    def send_down(j):
        d_own(0, j).start()
        d_own(1, j).start()

    def pass_down(j):
        d_own(0, j).wait_recv()
        d_own(1, j).wait_recv()
        d_forward(j).start()
        d_share(1, j).start()
        d_share(2, j).start()

    def share_down(j):
        d_forward(j).wait_recv()
        d_share(3, j).start()

    low = lax.broadcasted_iota(jnp.int32, (2 * TOK, 128), 1) < 64

    def activate(slots):
        inverse = lax.rsqrt(jnp.sum(ssq[...], axis=1, keepdims=True) * (1.0 / D) + 1e-06)
        for s in slots:
            base = s * 2 * HS
            gate = acc[:, base:base + 128] * inverse
            mid = acc[:, base + 128:base + 256] * inverse
            up = pltpu.roll(acc[:, base + 256:base + 384] * inverse, 64, 1)
            other = jnp.where(low, pltpu.roll(mid, 64, 1), up)
            main = (gate / (1.0 + jnp.exp(-gate)) * other).astype(BF16)
            tail = mid / (1.0 + jnp.exp(-mid)) * up
            hidden[s, :, 0:128] = main
            hidden[s, :, 128:192] = tail[:, 0:64].astype(BF16)
            packed_out[(0, 1, 2, 4)[s]] = main
            if s % 2 == 0:
                tail_two[...] = tail
            else:
                packed_out[s + 2] = jnp.where(low, tail_two[...], pltpu.roll(tail, 64, 1)).astype(BF16)

    def unpack():
        for to, start in ((0, TOK), (TOK, 0)):
            for s in range(NX):
                pair_hidden[s, to:to + TOK, 0:128] = packed_in[(0, 1, 2, 4)[s], start:start + TOK]
            for k in (3, 5):
                tails = packed_in[k, start:start + TOK].astype(F32)
                pair_hidden[k - 3, to:to + TOK, 128:192] = tails[:, 0:64].astype(BF16)
                pair_hidden[k - 2, to:to + TOK, 128:192] = pltpu.roll(tails, 64, 1)[:, 0:64].astype(BF16)

    def activate_near(j):
        activate(range(3))
        exchange(0).start()
        home_inv[...] = jnp.broadcast_to(
            lax.rsqrt(jnp.sum(home_ssq[...], axis=1, keepdims=True) * (1.0 / D) + 1e-06), (TOK, 128)
        )

    staged(J, [(0, 0, pick_rows), (1, 0, pass_rows), (0, 0, pass_weights), (2, 0, near_dots)])
    pass_rows(J - 1)
    each(ready_down, J2)
    send_down(0)
    send_down(1)
    staged(
        J,
        [(0, 0, share_far), (3 - J, J - 2, near_dots), (1, 0, far_dots), (4 - J, J - 1, activate_near)],
    )
    pass_down(0)
    send_down(2)
    far_dots(J - 1)
    activate((3,))
    exchange(1).start()
    pass_down(1)
    send_down(3)
    share_down(0)

    @pl.when(core == 0)
    def _():
        each(lambda j: core_down(j).wait_recv(), J2)

    def drain(j):
        relay(j).wait_send()
        for d in (1, 2, 3):
            dispatch(d, j).wait_send()
        to_pair(j).wait_send()

    def drain_ring(own, forward, share, j):
        own(0, j).wait_send()
        own(1, j).wait_send()
        forward(j).wait_send()
        for s in (1, 2, 3):
            share(s, j).wait_send()

    def drain_home(j):
        for copy in homes(j):
            copy.wait_send()

    def drain_second(j):
        drain_ring(d_own, d_forward, d_share, j)
        drain_home(j)

    each(drain)
    each(lambda j: drain_ring(g_own, g_forward, g_share, j))

    @pl.when(core == 1)
    def _():
        each(lambda j: pair_down(j).wait_send(), J2)
        each(lambda j: core_down(j).wait_send(), J2)

    def begin(g):
        parts = C // C2
        lanes = pl.ds(pl.multiple_of(g % parts * C2, C2), C2)
        residual = arrived[g // parts, :, lanes].astype(F32)
        normed = (residual * home_inv[:, 0:1] * gain[0:1, cols2(0, g)].astype(F32)).astype(BF16)
        start[g] = residual + zero_w[:, 0:1] * normed.astype(F32)

    each(begin, 2 * J2)
    exchange(0).wait_recv()
    exchange(1).wait_recv()
    unpack()
    exchange(0).wait_send()
    exchange(1).wait_send()

    def second_dots(j):
        for s in (1, 2, 3):
            d_share_in(s, j).wait_recv()
        total = jnp.dot(hidden[0], wd[j, 0, 0:HS, :], preferred_element_type=F32)
        total = total + jnp.dot(pair_hidden[0], wd[j, 0, HS:, :], preferred_element_type=F32)
        for s in range(1, NX):
            total = total + jnp.dot(hidden[s], wd[j, s, 0:HS, :], preferred_element_type=F32)
            total = total + jnp.dot(pair_hidden[s], wd[j, s, HS:, :], preferred_element_type=F32)
        home_out[j] = total.astype(BF16)
        for copy in homes(j)[::-1]:
            copy.start()
        keep_home(j).start()

    def finish(g):
        value = home_in[g]
        total = jnp.dot(combine_hi[...], value, preferred_element_type=F32)
        total = total + jnp.dot(combine_lo[...], value, preferred_element_type=F32)
        total = start[g] + total
        out_buf[g] = total.astype(BF16)
        store_out(g).start()

    def finish_mine(j):
        g = half * J2 + j
        keep_home(j).wait()
        for d in (1, 2, 3):
            home_arrival(d, g).wait_recv()
        finish(g)

    def finish_other(j):
        g = (1 - half) * J2 + j
        for d in (0, 1, 2, 3):
            home_arrival(d, g).wait_recv()
        finish(g)

    staged(
        J2 + 2,
        [
            (0, 0, second_dots), (-2, 2, pass_down), (-4, 4, send_down), (-1, 1, share_down),
            (2, 0, drain_second), (2, 0, finish_mine), (2, 0, finish_other),
        ],
        J2,
    )

    each(lambda j: store_out(j).wait(), 2 * J2)


def local(blocks, norm_gain, w_gate, w_up, w_down, route_ids, route_weights):
    anywhere = pl.BlockSpec(memory_space=pl.ANY)
    dma = pltpu.SemaphoreType.DMA
    return pl.pallas_call(
        kernel,
        out_shape=jax.ShapeDtypeStruct(blocks.shape, blocks.dtype),
        in_specs=[anywhere] * 7,
        out_specs=anywhere,
        scratch_shapes=[
            pltpu.VMEM((1, D), BF16),
            pltpu.VMEM((2, TOK), jnp.int32),
            pltpu.VMEM((2, TOK), F32),
            pltpu.VMEM((J, TOK, C), BF16),
            pltpu.VMEM((J, TOK, C), BF16),
            pltpu.VMEM((J, 2 * TOK, C), BF16),
            pltpu.VMEM((J, NX, 2 * HS, C), BF16),
            pltpu.VMEM((J2, NX, 2 * HS, C2), BF16),
            pltpu.VMEM((J, 2 * TOK, C), BF16),
            pltpu.VMEM((2 * TOK, NX * 2 * HS), F32),
            pltpu.VMEM((2 * TOK, 128), F32),
            pltpu.VMEM((TOK, 128), F32),
            pltpu.VMEM((NX, 2 * TOK, HS), BF16),
            pltpu.VMEM((NX, 2 * TOK, HS), BF16),
            pltpu.VMEM((6, 2 * TOK, 128), BF16),
            pltpu.VMEM((6, 2 * TOK, 128), BF16),
            pltpu.VMEM((2 * TOK, 128), F32),
            pltpu.VMEM((J2, 2 * TOK, C2), BF16),
            pltpu.VMEM((2 * J2, TOK, C2), BF16),
            pltpu.VMEM((2 * J2, TOK, C2), F32),
            pltpu.VMEM((2 * J2, TOK, C2), BF16),
            pltpu.VMEM((TOK, TOK), BF16),
            pltpu.VMEM((TOK, TOK), BF16),
            pltpu.VMEM((TOK, TOK), BF16),
            pltpu.VMEM((TOK, 128), F32),
            pltpu.VMEM((TOK, 128), F32),
            dma((3,)), dma((3, J)), dma((2 * J2,)), dma((2 * J2,)),
            dma((J,)), dma((J,)), dma((3, J)), dma((3, J)), dma((J,)), dma((J,)),
            dma((2, J)), dma((2, J)), dma((J,)), dma((J,)), dma((3, J)), dma((3, J)),
            dma((2, J2)), dma((2, J2)), dma((J2,)), dma((J2,)), dma((3, J2)), dma((3, J2)),
            dma((J2,)), dma((J2,)), dma((J2,)), dma((J2,)), dma((2,)), dma((2,)),
            dma((7, J2)), dma((4, 2 * J2)),
        ],
        compiler_params=pltpu.CompilerParams(
            collective_id=0, has_side_effects=True, vmem_limit_bytes=60 * 1024 * 1024
        ),
        cost_estimate=pl.CostEstimate(
            flops=2 * 3 * 1024 * D * HS, bytes_accessed=6 * 1024 * 1024, transcendentals=256 * 768
        ),
    )(
        blocks, norm_gain, jnp.swapaxes(w_gate, 1, 2), jnp.swapaxes(w_up, 1, 2), w_down,
        jnp.swapaxes(route_ids, 1, 2), jnp.swapaxes(route_weights, 1, 2),
    )


def solution(mesh):
    placed = (
        P("section", ("dp", "expert"), None),
        P("section", None),
        P("section", None, "expert"),
        P("section", None, "expert"),
        P("section", "expert", None),
        P("section", ("dp", "expert"), None),
        P("section", ("dp", "expert"), None),
    )
    return jax.shard_map(
        local,
        mesh=mesh,
        in_specs=placed,
        out_specs=P("section", ("dp", "expert"), None),
        check_vma=False,
    )
```
